512 devices in a mesh: seg: 16 (over x, z_lo), space: 32 (over z_hi, y, core).
Axes of the slice: x: 4, y: 8, z: 8 (z_hi: 2, z_lo: 4; z = z_hi * 4 + z_lo), core: 2. Of those that a mesh axis runs over, the one named last changes fastest.
Arguments:
- basis: bfloat16 [16, 8, 1024, 1024], P('seg', None, 'space'), may hold values from -16 to 16
- base_grad: bfloat16 [16, 2, 2, 1024, 1024], P('seg', None, None, 'space'), may hold values from -8 to 8
- step_counts: int32 [16], P('seg'), may hold values from 2 to 8
- shift: int32 [2], replicated, may hold values from 0 to 1023
Outputs:
- new_vector: float32 [16, 1024, 1024], P('seg', 'space')
- hessenberg: float32 [9], replicated
The draws below stay inside these ranges and needn't reach their ends.
All inputs are finite; a program needn't handle non-finite values.
Results may differ from the reference program's by a relative error of at most 0.0003.
Values may be sent and summed in bfloat16 or wider, within the bound.
A program may use at most 64 MiB of HBM per device.

```python
import jax
import jax.numpy as jnp
from jax import lax

GRID = 1024
KRYLOV = 8
STEPS = 1
SEGS = 16


def draw_basis(key, part):
    key = jax.random.fold_in(key, 7)
    key_rough, key_common, key_weight = jax.random.split(key, 3)
    segment_pos = (jnp.arange(SEGS, dtype=jnp.float32) + 0.5) / SEGS
    row_pos = (jnp.arange(GRID, dtype=jnp.float32) + 0.5) / GRID
    rough = jax.random.normal(key_rough, (SEGS, KRYLOV, GRID, GRID), jnp.float32)
    common = jax.random.normal(key_common, (GRID, GRID), jnp.float32)
    scales = 10.0 ** (0.5 * segment_pos[:, None, None, None] + 0.5 * row_pos[None, None, :, None])
    weights = jax.random.uniform(key_weight, (KRYLOV,), jnp.float32, 0.3, 0.8)[None, :, None, None]
    values = scales * (weights * common[None, None] + jnp.sqrt(1.0 - weights * weights) * rough) * 0.25
    return jnp.clip(values, -16.0, 16.0).astype(jnp.bfloat16)


def place_ends(values, stream_key, least, largest):
    shape = values.shape
    spot = [jax.random.randint(jax.random.fold_in(stream_key, axis), (), 0, shape[axis]) for axis in range(len(shape))]
    values = values.at[tuple(spot)].set(least)
    longest = shape.index(max(shape))
    spot[longest] = (spot[longest] + 1) % shape[longest]
    return values.at[tuple(spot)].set(largest)


def steps_of(key, extent, cuts, least, high):
    gain, own = 1.0, jax.random.fold_in(key, 6)
    for axis_at, blocks in cuts:
        draws = jnp.exp(jax.random.uniform(jax.random.fold_in(own, axis_at), (blocks,), jnp.float32, least / len(cuts), high / len(cuts)))
        gain = gain * jnp.repeat(draws, extent[axis_at] // blocks).reshape([-1 if axis == axis_at else 1 for axis in range(len(extent))])
    return gain


def gaussian(key, dims, spread, most, cuts=(), kind=jnp.bfloat16):
    result = spread * jax.random.normal(key, dims, jnp.float32)
    if cuts:
        result = result * steps_of(key, dims, cuts, -0.22, 0.18)
    return jnp.clip(result, -most, most).astype(kind)


def setup_inputs(seed: int = 0) -> dict:
    key_list = jax.random.split(jax.random.key(seed), 5)
    basis = draw_basis(jax.random.fold_in(key_list[4], 71), 0)
    base_grad = gaussian(key_list[1], (SEGS, STEPS + 1, 2, GRID, GRID), 2.0, 8.0, ((0, 16), (3, 32)))
    step_counts = place_ends(jax.random.randint(key_list[2], (SEGS,), 2, 9), jax.random.fold_in(key_list[2], 1), 2, 8).astype(jnp.int32)
    shift = jax.random.randint(key_list[3], (2,), 0, GRID).astype(jnp.int32)
    return {"basis": basis, "base_grad": base_grad, "step_counts": step_counts, "shift": shift}


def phi_pair(scaled):
    small = jnp.abs(scaled) < 0.5
    safe = jnp.where(small, jnp.ones_like(scaled), scaled)
    growth = jnp.expm1(safe)
    first_phi = growth / safe
    second_phi = (growth - safe) / (safe * safe)
    series_one = jnp.zeros_like(scaled)
    series_two = jnp.zeros_like(scaled)
    for power in range(10, -1, -1):
        fact_one = 1.0
        for factor in range(2, power + 2):
            fact_one = fact_one * factor
        fact_two = fact_one * (power + 2)
        series_one = series_one * scaled + 1.0 / fact_one
        series_two = series_two * scaled + 1.0 / fact_two
    return (jnp.exp(scaled), jnp.where(small, series_one, first_phi), jnp.where(small, series_two, second_phi))

def reference(basis, base_grad, step_counts, shift):
    length = basis.shape[2]
    freq = jnp.arange(length, dtype=jnp.int32)
    signed = jnp.where(freq < length // 2, freq, freq - length)
    wave = signed.astype(jnp.float32) * (8.0 / length)
    deriv = jnp.where(signed == -(length // 2), jnp.zeros_like(wave), wave)
    squared = wave[:, None] ** 2 + wave[None, :] ** 2
    linear = squared - squared * squared
    deriv_x = deriv[:, None]
    deriv_y = deriv[None, :]

    def flow_one(packed_args):
        start_bf, grads, counted = packed_args
        start = start_bf.astype(jnp.float32)
        step_size = 0.01 * counted.astype(jnp.float32)
        decay, phi_one, phi_two = phi_pair(linear * step_size)

        def nonlinear(spectrum, section_index):
            grad_x = jnp.fft.ifft2(1j * deriv_x * spectrum).real
            grad_y = jnp.fft.ifft2(1j * deriv_y * spectrum).real
            term = -(grads[section_index, 0].astype(jnp.float32) * grad_x + grads[section_index, 1].astype(jnp.float32) * grad_y)
            return jnp.fft.fft2(term)
        state = jnp.fft.fft2(start)
        for section_index in range(STEPS):
            now_term = nonlinear(state, section_index)
            middle = decay * state + step_size * phi_one * now_term
            state = middle + step_size * phi_two * (nonlinear(middle, section_index + 1) - now_term)
        return jnp.fft.ifft2(state).real.astype(start.dtype)
    flowed = lax.map(flow_one, (basis[:, -1], base_grad, step_counts))
    rolled = jnp.roll(flowed[-1], (shift[0], shift[1]), axis=(0, 1))
    flowed = flowed.at[-1].set(rolled)
    residual_in = jnp.roll(flowed, 1, axis=0) - basis[:, -1].astype(jnp.float32)
    cells = basis.shape[0] * length * length
    coeffs = jnp.stack([jnp.sum(basis[:, index].astype(jnp.float32) * residual_in) for index in range(KRYLOV)]) / cells
    remainder = residual_in
    for index in range(KRYLOV):
        remainder = remainder - coeffs[index] * basis[:, index].astype(jnp.float32)
    norm_value = jnp.sqrt(jnp.sum(remainder * remainder) / cells)
    return (remainder / norm_value, jnp.concatenate([coeffs, norm_value[None]]))
```

```python
import math

import jax
import jax.numpy as jnp
import ml_dtypes
import numpy as np
from jax import lax
from jax.experimental import pallas as pl
from jax.experimental.pallas import tpu as pltpu
from jax.sharding import PartitionSpec as P

MESH = pl.DeviceIdType.MESH
GRID = 1024
SPACE = 32
SEGS = 16
KRYLOV = 8
ROWS = GRID // SPACE
HALF = math.sqrt(0.5)


def make_tables():
    tabs = {}
    small = np.arange(128)
    full = np.arange(256)
    short = np.arange(32)

    def by_owner(real, imag):
        parts = [part.reshape(part.shape[0], 32, 4) for part in (real, imag)]
        return np.stack(parts, axis=2).reshape(real.shape[0], 256)

    def owner_rows(real, imag):
        parts = [part.reshape(32, 4, -1) for part in (real, imag)]
        return np.stack(parts, axis=1).reshape(256, -1)

    def swapped(table):
        parts = table.reshape(32, 2, 4, 256)
        return np.stack([parts[:, 1], -parts[:, 0]], axis=1).reshape(256, 256)

    angle = 2 * np.pi / 256 * ((full[:, None] * small[None, :]) % 256)
    real, imag = np.cos(angle), -np.sin(angle)
    imag[:, 0] = (-1.0) ** full
    tabs["A0"] = by_owner(real, imag)
    real, imag = 2 * np.cos(angle.T), -2 * np.sin(angle.T)
    real[0], imag[0] = 1.0, (-1.0) ** full
    tabs["B0"] = owner_rows(real, imag) / GRID
    angle = 2 * np.pi / 128 * ((small[:, None] * small[None, :]) % 128)
    cos, sin = np.cos(angle), np.sin(angle)
    tabs["A1"] = np.concatenate([by_owner(cos, -sin), by_owner(sin, cos)], 0)
    real = np.concatenate([cos, sin], 1)
    imag = np.concatenate([-sin, cos], 1)
    tabs["B1"] = owner_rows(real, imag) * 2 / GRID
    tabs["D0"] = swapped(tabs["B0"])
    tabs["D1"] = swapped(tabs["B1"])
    angle = 2 * np.pi / 32 * ((short[:, None] * short[None, :]) % 32)
    cos, sin = np.cos(angle), np.sin(angle)
    table = np.zeros((2, 5, 32, 32, 2, 4))
    for low in range(4):
        table[0, low, :, :, 0, low] = cos
        table[0, low, :, :, 1, low] = sin
        table[1, low, :, :, 0, low] = -sin
        table[1, low, :, :, 1, low] = cos
    table[0, 4, :, :, 1, 0] = cos
    table[1, 4, :, :, 1, 0] = -sin
    tabs["L1"] = table.reshape(320, 256)
    table = np.zeros((32, 2, 4, 2, 4, 32))
    for low in range(4):
        table[:, 0, low, 0, low, :] = cos
        table[:, 0, low, 1, low, :] = -sin
        table[:, 1, low, 0, low, :] = sin
        table[:, 1, low, 1, low, :] = cos
    tabs["M1"] = table.reshape(256, 256) / GRID
    for name, sign in (("L2", 1.0), ("M2", -1.0)):
        table = np.zeros((2, 4, 32, 2, 4, 32))
        for slot in range(4):
            table[0, slot, :, 0, slot, :] = cos
            table[0, slot, :, 1, slot, :] = -sign * sin
            table[1, slot, :, 0, slot, :] = sign * sin
            table[1, slot, :, 1, slot, :] = cos
        tabs[name] = table.reshape(256, 256)
    return tabs


def make_constants():
    offsets, parts, at = {}, [], 0
    for name, table in make_tables().items():
        table = table.astype(np.float32)
        high = table.astype(ml_dtypes.bfloat16)
        low = (table - high.astype(np.float32)).astype(ml_dtypes.bfloat16)
        count = table.shape[0]
        offsets[name] = (at, count)
        parts += [high, low]
        at += 2 * count
    small = np.arange(128)
    short = np.arange(32)
    twist = np.zeros((96, 128))
    angle = 2 * np.pi / GRID * ((np.arange(1, 4)[:, None] * small[None, :]) % GRID)
    twist[0:3], twist[8:11] = np.cos(angle), np.sin(angle)
    angle = 2 * np.pi / GRID * ((short[:, None] * short[None, :]) % GRID)
    twist[16:48] = np.tile(np.cos(angle), (1, 4))
    twist[48:80] = np.tile(np.sin(angle), (1, 4))
    for slot in range(4):
        freq = 4 * small if slot == 0 else slot + 8 * small
        freq = np.where(freq < GRID // 2, freq, freq - GRID) * (8.0 / GRID)
        lanes = np.stack([freq.reshape(32, 4)] * 2, axis=1).reshape(256)
        twist[80 + slot], twist[88 + slot] = lanes[:128], lanes[128:]
    return offsets, np.concatenate(parts, 0), twist.astype(np.float32)


OFFSETS, TABLE, TWIST = make_constants()


def dot(left, right):
    return jnp.dot(left, right, preferred_element_type=jnp.float32)


def halves(value):
    high = value.astype(jnp.bfloat16)
    return high, (value - high.astype(jnp.float32)).astype(jnp.bfloat16)


def phi_triple(scaled):
    small = jnp.abs(scaled) < 0.5
    safe = jnp.where(small, jnp.ones_like(scaled), scaled)
    inverse = 1.0 / safe
    growth = jnp.exp(safe) - 1.0
    first_phi = growth * inverse
    second_phi = (first_phi - 1.0) * inverse
    series_one = jnp.zeros_like(scaled)
    series_two = jnp.zeros_like(scaled)
    for power in range(10, -1, -1):
        fact_one = float(math.factorial(power + 1))
        series_one = series_one * scaled + 1.0 / fact_one
        series_two = series_two * scaled + 1.0 / (fact_one * (power + 2))
    return (
        jnp.exp(scaled),
        jnp.where(small, series_one, first_phi),
        jnp.where(small, series_two, second_phi),
    )


def kernel(
    steps_ref, shift_ref, basis_hbm, grad_hbm, table_hbm, twist_hbm,
    out_ref, hess_ref,
    basis, grad, table, twist,
    s1, s2, s3, s4, s5, s6, r1, r2, r3, r4, r5, r6,
    mine, sum_a, sum_b,
    local_sem, send_sem, recv_sem, ready,
):
    seg = lax.axis_index("seg")
    me = lax.axis_index("space")
    f32 = jnp.float32

    loads = [
        pltpu.make_async_copy(source, target, local_sem.at[at])
        for at, (source, target) in enumerate(
            ((basis_hbm, basis), (twist_hbm, twist), (table_hbm, table), (grad_hbm, grad))
        )
    ]
    for load in loads:
        load.start()

    barrier = pltpu.get_barrier_semaphore()

    def greet_space(step, carry):
        peer = lax.rem(me + step, SPACE)
        pl.semaphore_signal(barrier, inc=1, device_id={"space": peer}, device_id_type=MESH)
        return carry

    def greet_seg(step, carry):
        peer = lax.rem(seg + step, SEGS)
        pl.semaphore_signal(barrier, inc=1, device_id={"seg": peer}, device_id_type=MESH)
        return carry

    lax.fori_loop(1, SPACE, greet_space, 0)
    lax.fori_loop(1, SEGS, greet_seg, 0)

    def const(name):
        at, count = OFFSETS[name]
        return table[at : at + count, :], table[at + count : at + 2 * count, :]

    def const_left(name, value):
        high, low = halves(value)
        table_high, table_low = const(name)
        both = dot(table_high, jnp.concatenate([high, low], axis=1))
        return both[:, :128] + both[:, 128:] + dot(table_low, high)

    def const_right(value, name):
        count = value.shape[0]
        high, low = halves(value)
        table_high, table_low = const(name)
        both = dot(jnp.concatenate([high, low], axis=0), table_high)
        return both[:count] + both[count:] + dot(high, table_low)

    def send(source, target, at, rows):
        def step_to(step, carry):
            peer = lax.rem(me + step, SPACE)
            pltpu.make_async_remote_copy(
                src_ref=source.at[pl.ds(pl.multiple_of(peer * rows, 8), rows)],
                dst_ref=target.at[pl.ds(pl.multiple_of(me * rows, 8), rows)],
                send_sem=send_sem.at[at],
                recv_sem=recv_sem.at[at],
                device_id={"space": peer},
                device_id_type=MESH,
            ).start()
            return carry

        lax.fori_loop(1, SPACE, step_to, 0)
        own = pl.ds(pl.multiple_of(me * rows, 8), rows)
        target[own, :] = source[own, :]

    def arrival(source, target, at, rows):
        return pltpu.make_async_remote_copy(
            src_ref=source.at[pl.ds(0, rows)],
            dst_ref=target.at[pl.ds(0, rows)],
            send_sem=send_sem.at[at],
            recv_sem=recv_sem.at[at],
            device_id={"space": me},
            device_id_type=MESH,
        )

    def row_spectrum(field):
        group = [field[:, 128 * at : 128 * at + 128] for at in range(8)]
        plus = [group[at] + group[at + 4] for at in range(4)]
        minus = [group[at] - group[at + 4] for at in range(4)]
        zero = jnp.concatenate([plus[0] + plus[2], plus[1] + plus[3]], axis=1)
        inner = HALF * (minus[1] - minus[3])
        outer = HALF * (minus[1] + minus[3])
        pairs = (
            (minus[0] + inner, -(minus[2] + outer)),
            (plus[0] - plus[2], plus[3] - plus[1]),
            (minus[0] - inner, minus[2] - outer),
        )
        rest = []
        for at, (real, imag) in enumerate(pairs):
            cos, sin = twist[at : at + 1, :], twist[8 + at : 9 + at, :]
            rest.append(
                jnp.concatenate([real * cos + imag * sin, imag * cos - real * sin], axis=1)
            )
        return const_right(zero, "A0"), const_right(jnp.concatenate(rest, axis=0), "A1")

    def row_field(zero, rest):
        turned = []
        for at in range(3):
            real, imag = rest[32 * at : 32 * at + 32, :128], rest[32 * at : 32 * at + 32, 128:]
            cos, sin = twist[at : at + 1, :], twist[8 + at : 9 + at, :]
            turned.append((real * cos - imag * sin, real * sin + imag * cos))
        (re1, im1), (re2, im2), (re3, im3) = turned
        even, odd = zero[:, :128], zero[:, 128:]
        sums = (even + re2, odd - im2, even - re2, odd + im2)
        differences = (
            re1 + re3,
            HALF * ((re1 - im1) - (re3 + im3)),
            im3 - im1,
            HALF * ((re3 - im3) - (re1 + im1)),
        )
        pieces = [sums[at] + differences[at] for at in range(4)]
        pieces += [sums[at] - differences[at] for at in range(4)]
        return jnp.concatenate(pieces, axis=1)

    def rows_forward(field, target):
        zero, rest = row_spectrum(field)
        target[...] = jnp.concatenate([zero, rest], axis=0).T
        return zero, rest

    def rows_inverse(received):
        turned = received.T
        return row_field(const_right(turned[:32], "B0"), const_right(turned[32:], "B1"))

    def stacked(value):
        return jnp.concatenate([value] * 5, axis=0)

    lane = lax.broadcasted_iota(jnp.int32, (160, 128), 1)
    row = lax.broadcasted_iota(jnp.int32, (160, 128), 0)
    anchor = jnp.where((lane[:32] < 32) & (me == 0), 1.0, 0.0).astype(f32)

    def columns_forward(received):
        value = const_left("L1", received)
        real, imag = value[:160], value[160:]
        real = jnp.concatenate([real[:32] + anchor * imag[128:], real[32:]], axis=0)
        imag = jnp.concatenate([imag[:32] - anchor * value[128:160], imag[32:]], axis=0)
        cos, sin = stacked(twist[16:48, :]), stacked(twist[48:80, :])
        turned = jnp.concatenate([real * cos + imag * sin, imag * cos - real * sin], axis=1)
        value = const_right(turned, "L2")
        return value[:, :128], value[:, 128:]

    def columns_inverse(real, imag):
        value = const_right(jnp.concatenate([real, imag], axis=1), "M2")
        real, imag = value[:, :128], value[:, 128:]
        cos, sin = stacked(twist[16:48, :]), stacked(twist[48:80, :])
        real, imag = real * cos - imag * sin, real * sin + imag * cos
        value = jnp.concatenate(
            [real[:32] - anchor * imag[128:], real[32:128], imag[:32] + anchor * real[128:], imag[32:128]],
            axis=0,
        )
        return const_left("M1", value)

    loads[0].wait()
    loads[1].wait()
    loads[2].wait()
    start = basis[KRYLOV - 1].astype(f32)
    zero, rest = rows_forward(start, s1)
    pl.semaphore_wait(barrier, SPACE + SEGS - 2)
    pl.semaphore_signal(
        ready, inc=1, device_id={"seg": lax.rem(seg + SEGS - 1, SEGS)}, device_id_type=MESH
    )
    send(s1, r1, 0, 8)

    waves = [
        jnp.concatenate([twist[80 + at : 81 + at, :], twist[88 + at : 89 + at, :]], axis=1)
        for at in range(4)
    ]
    lifted = jnp.concatenate([rest[32 * at : 32 * at + 32] * waves[at + 1] for at in range(3)], axis=0)
    grad_y = row_field(const_right(zero * waves[0], "D0"), const_right(lifted, "D1"))

    slot = lane // 32
    low = row // 32
    freq_x = row % 32 + 32 * (lane % 32)
    base = 4 * me + low
    freq_y = jnp.where(low == 4, GRID // 2, jnp.where(slot == 0, 4 * base, slot + 8 * base))
    signed_x = jnp.where(freq_x < GRID // 2, freq_x, freq_x - GRID)
    signed_y = jnp.where(freq_y < GRID // 2, freq_y, freq_y - GRID)
    wave_x = signed_x.astype(f32) * (8.0 / GRID)
    wave_y = signed_y.astype(f32) * (8.0 / GRID)
    deriv_x = jnp.where(signed_x == -(GRID // 2), 0.0, wave_x)
    deriv_y = jnp.where(signed_y == -(GRID // 2), 0.0, wave_y)
    squared = wave_x * wave_x + wave_y * wave_y
    step_size = 0.01 * steps_ref[0].astype(f32)
    decay, phi_one, phi_two = phi_triple((squared - squared * squared) * step_size)
    phi_one = step_size * phi_one
    phi_two = step_size * phi_two

    done = arrival(s1, r1, 0, 248)
    done.wait_recv()
    state_re, state_im = columns_forward(r1[...])

    s2[...] = columns_inverse(-deriv_x * state_im, deriv_x * state_re)
    send(s2, r2, 1, 8)
    loads[3].wait()
    part_y = grad[1].astype(f32) * grad_y
    part_x = -grad[0].astype(f32)
    arrival(s2, r2, 1, 248).wait_recv()
    term = part_x * rows_inverse(r2[...]) - part_y

    rows_forward(term, s3)
    send(s3, r3, 2, 8)
    flat = basis[...].reshape(KRYLOV * ROWS, GRID)
    gram = lax.dot_general(flat, flat, (((1,), (1,)), ((), ())), preferred_element_type=f32)
    gram_row = lax.broadcasted_iota(jnp.int32, (256, 256), 0)
    gram_lane = lax.broadcasted_iota(jnp.int32, (256, 256), 1)
    gram = jnp.where(gram_row % 32 == gram_lane % 32, gram, 0.0)
    gram = jnp.concatenate(
        [jnp.sum(gram[32 * at : 32 * at + 32], axis=0, keepdims=True) for at in range(8)], axis=0
    )
    spot_row = lax.broadcasted_iota(jnp.int32, (8, 128), 0)
    spot_lane = lax.broadcasted_iota(jnp.int32, (8, 128), 1)
    gram_sums = jnp.zeros((8, 128), f32)
    for at in range(8):
        part = jnp.sum(jnp.where(gram_lane[:8] // 32 == at, gram, 0.0), axis=1, keepdims=True)
        gram_sums = gram_sums + jnp.where(spot_lane == 16 + 8 * spot_row + at, part, 0.0)
    gram_sums = jnp.sum(gram_sums, axis=0, keepdims=True)
    arrival(s3, r3, 2, 248).wait_recv()
    term_re, term_im = columns_forward(r3[...])
    middle_re = decay * state_re + phi_one * term_re
    middle_im = decay * state_im + phi_one * term_im

    toward_x = columns_inverse(-deriv_x * middle_im, deriv_x * middle_re)
    toward_y = columns_inverse(-deriv_y * middle_im, deriv_y * middle_re)
    for peer in range(SPACE):
        s4[16 * peer : 16 * peer + 8, :] = toward_x[8 * peer : 8 * peer + 8]
        s4[16 * peer + 8 : 16 * peer + 16, :] = toward_y[8 * peer : 8 * peer + 8]
    send(s4, r4, 3, 16)
    offset = (freq_x * shift_ref[0] + freq_y * shift_ref[1]) & (GRID - 1)
    angle = (2.0 * math.pi / GRID) * offset.astype(f32)
    is_last = seg == SEGS - 1
    cosine = jnp.where(is_last, jnp.cos(angle), 1.0)
    sine = jnp.where(is_last, jnp.sin(angle), 0.0)
    arrival(s4, r4, 3, 496).wait_recv()
    got_x = jnp.concatenate([r4[16 * peer : 16 * peer + 8, :] for peer in range(SPACE)], axis=0)
    got_y = jnp.concatenate([r4[16 * peer + 8 : 16 * peer + 16, :] for peer in range(SPACE)], axis=0)
    term = -(grad[2].astype(f32) * rows_inverse(got_x) + grad[3].astype(f32) * rows_inverse(got_y))

    rows_forward(term, s5)
    send(s5, r5, 4, 8)
    kept_re = middle_re - phi_two * term_re
    kept_im = middle_im - phi_two * term_im
    arrival(s5, r5, 4, 248).wait_recv()
    term_re, term_im = columns_forward(r5[...])
    state_re = kept_re + phi_two * term_re
    state_im = kept_im + phi_two * term_im

    s6[...] = columns_inverse(cosine * state_re + sine * state_im, cosine * state_im - sine * state_re)
    pl.semaphore_wait(ready, 1)
    next_seg = lax.rem(seg + 1, SEGS)

    def onward(step, carry):
        peer = lax.rem(me + step, SPACE)
        pltpu.make_async_remote_copy(
            src_ref=s6.at[pl.ds(pl.multiple_of(peer * 8, 8), 8)],
            dst_ref=r6.at[pl.ds(pl.multiple_of(me * 8, 8), 8)],
            send_sem=send_sem.at[5],
            recv_sem=recv_sem.at[5],
            device_id={"seg": next_seg, "space": peer},
            device_id_type=MESH,
        ).start()
        return carry

    lax.fori_loop(0, SPACE, onward, 0)
    arrival(s6, r6, 5, 256).wait_recv()
    wrapped = rows_inverse(r6[...]) - start

    def folded(value):
        total = value[:, :128]
        for at in range(1, 8):
            total = total + value[:, 128 * at : 128 * at + 128]
        return jnp.sum(total, axis=0, keepdims=True)

    lines = [folded(wrapped * basis[at].astype(f32)) for at in range(KRYLOV)]
    lines.append(folded(wrapped * wrapped))
    lines.append(jnp.zeros((7, 128), f32))
    sums = jnp.sum(jnp.concatenate(lines, axis=0), axis=1, keepdims=True)
    spot_row = lax.broadcasted_iota(jnp.int32, (16, 128), 0)
    spot_lane = lax.broadcasted_iota(jnp.int32, (16, 128), 1)
    line = jnp.sum(jnp.where(spot_row == spot_lane, sums, 0.0), axis=0, keepdims=True) + gram_sums

    def spread(target, axis, count, own, at):
        target[own] = mine[at]

        def step_to(step, carry):
            peer = lax.rem(own + step, count)
            pltpu.make_async_remote_copy(
                src_ref=mine.at[at],
                dst_ref=target.at[own],
                send_sem=send_sem.at[6 + at],
                recv_sem=recv_sem.at[6 + at],
                device_id={axis: peer},
                device_id_type=MESH,
            ).start()
            return carry

        lax.fori_loop(1, count, step_to, 0)
        done = pltpu.make_async_remote_copy(
            src_ref=target.at[pl.ds(0, count - 1)],
            dst_ref=target.at[pl.ds(0, count - 1)],
            send_sem=send_sem.at[6 + at],
            recv_sem=recv_sem.at[6 + at],
            device_id={axis: own},
            device_id_type=MESH,
        )
        done.wait_recv()
        return done, jnp.sum(target[...], axis=0)

    mine[0] = line
    sent_a, line = spread(sum_a, "space", SPACE, me, 0)
    mine[1] = line
    sent_b, line = spread(sum_b, "seg", SEGS, seg, 1)
    line = line * (1.0 / (SEGS * GRID * GRID))

    lanes = lax.broadcasted_iota(jnp.int32, (1, 128), 1)

    def lane_of(at):
        return jnp.sum(jnp.where(lanes == at, line, 0.0), axis=1, keepdims=True)

    coeffs = [lane_of(at) for at in range(KRYLOV)]
    norm_sq = lane_of(KRYLOV)
    left = jnp.zeros((1, 128), f32)
    right = jnp.zeros((1, 128), f32)
    for at in range(KRYLOV):
        left = left + jnp.where((lanes >= 16 + 8 * at) & (lanes < 24 + 8 * at), coeffs[at], 0.0)
        right = right + jnp.where((lanes >= 16) & (lanes % 8 == at) & (lanes < 80), coeffs[at], 0.0)
        norm_sq = norm_sq - 2.0 * coeffs[at] * coeffs[at]
    norm_sq = norm_sq + jnp.sum(left * right * line, axis=1, keepdims=True)
    norm = jnp.sqrt(norm_sq)
    hess_ref[...] = jnp.where(lanes == KRYLOV, norm, line)
    inverse = 1.0 / norm
    remainder = wrapped
    for at in range(KRYLOV):
        remainder = remainder - coeffs[at] * basis[at].astype(f32)
    out_ref[0] = remainder * inverse

    for source, at, rows in ((s1, 0, 248), (s2, 1, 248), (s3, 2, 248), (s4, 3, 496), (s5, 4, 248), (s6, 5, 256)):
        arrival(source, source, at, rows).wait_send()
    sent_a.wait_send()
    sent_b.wait_send()


def per_device(basis, base_grad, step_counts, shift):
    any_space = pl.BlockSpec(memory_space=pl.ANY)
    scalars = pl.BlockSpec(memory_space=pltpu.SMEM)
    f32, bf16 = jnp.float32, jnp.bfloat16
    tile = pltpu.VMEM((256, 128), f32)
    wide = pltpu.VMEM((512, 128), f32)
    new_vector, line = pl.pallas_call(
        kernel,
        out_shape=(
            jax.ShapeDtypeStruct((1, ROWS, GRID), f32),
            jax.ShapeDtypeStruct((1, 128), f32),
        ),
        in_specs=[scalars, scalars] + [any_space] * 4,
        out_specs=(pl.BlockSpec(memory_space=pltpu.VMEM),) * 2,
        scratch_shapes=[
            pltpu.VMEM((KRYLOV, ROWS, GRID), bf16),
            pltpu.VMEM((4, ROWS, GRID), bf16),
            pltpu.VMEM(TABLE.shape, bf16),
            pltpu.VMEM(TWIST.shape, f32),
            tile, tile, tile, wide, tile, tile,
            tile, tile, tile, wide, tile, tile,
            pltpu.VMEM((2, 1, 128), f32),
            pltpu.VMEM((SPACE, 1, 128), f32),
            pltpu.VMEM((SEGS, 1, 128), f32),
            pltpu.SemaphoreType.DMA((4,)),
            pltpu.SemaphoreType.DMA((8,)),
            pltpu.SemaphoreType.DMA((8,)),
            pltpu.SemaphoreType.REGULAR,
        ],
        compiler_params=pltpu.CompilerParams(
            collective_id=0, has_side_effects=True, vmem_limit_bytes=40 * 1024 * 1024
        ),
    )(
        step_counts,
        shift,
        basis[0],
        base_grad.reshape(4, ROWS, GRID),
        jnp.asarray(TABLE),
        jnp.asarray(TWIST),
    )
    return new_vector, line[0, : KRYLOV + 1]


def solution(mesh):
    in_specs = (P("seg", None, "space", None), P("seg", None, None, "space", None), P("seg"), P())
    out_specs = (P("seg", "space", None), P())
    return jax.shard_map(
        per_device, mesh=mesh, in_specs=in_specs, out_specs=out_specs, check_vma=False
    )
```

```python
import math

import jax
import jax.numpy as jnp
import ml_dtypes
import numpy as np
from jax import lax
from jax.experimental import pallas as pl
from jax.experimental.pallas import tpu as pltpu
from jax.sharding import PartitionSpec as P

MESH = pl.DeviceIdType.MESH
GRID = 1024
SPACE = 32
SEGS = 16
KRYLOV = 8
PLANE = 32
COLUMN = 16
ROWS = GRID // SPACE
HALF = math.sqrt(0.5)


def make_tables():
    tabs = {}
    small = np.arange(128)
    full = np.arange(256)
    short = np.arange(32)

    def by_owner(real, imag):
        parts = [part.reshape(part.shape[0], 32, 4) for part in (real, imag)]
        return np.stack(parts, axis=2).reshape(real.shape[0], 256)

    def owner_rows(real, imag):
        parts = [part.reshape(32, 4, -1) for part in (real, imag)]
        return np.stack(parts, axis=1).reshape(256, -1)

    def swapped(table):
        parts = table.reshape(32, 2, 4, 256)
        return np.stack([parts[:, 1], -parts[:, 0]], axis=1).reshape(256, 256)

    angle = 2 * np.pi / 256 * ((full[:, None] * small[None, :]) % 256)
    real, imag = np.cos(angle), -np.sin(angle)
    imag[:, 0] = (-1.0) ** full
    tabs["A0"] = by_owner(real, imag)
    real, imag = 2 * np.cos(angle.T), -2 * np.sin(angle.T)
    real[0], imag[0] = 1.0, (-1.0) ** full
    tabs["B0"] = owner_rows(real, imag) / GRID
    angle = 2 * np.pi / 128 * ((small[:, None] * small[None, :]) % 128)
    cos, sin = np.cos(angle), np.sin(angle)
    tabs["A1"] = np.concatenate([by_owner(cos, -sin), by_owner(sin, cos)], 0)
    real = np.concatenate([cos, sin], 1)
    imag = np.concatenate([-sin, cos], 1)
    tabs["B1"] = owner_rows(real, imag) * 2 / GRID
    tabs["D0"] = swapped(tabs["B0"])
    tabs["D1"] = swapped(tabs["B1"])
    angle = 2 * np.pi / 32 * ((short[:, None] * short[None, :]) % 32)
    cos, sin = np.cos(angle), np.sin(angle)
    table = np.zeros((2, 5, 32, 32, 2, 4))
    for low in range(4):
        table[0, low, :, :, 0, low] = cos
        table[0, low, :, :, 1, low] = sin
        table[1, low, :, :, 0, low] = -sin
        table[1, low, :, :, 1, low] = cos
    table[0, 4, :, :, 1, 0] = cos
    table[1, 4, :, :, 1, 0] = -sin
    tabs["L1"] = table.reshape(320, 256)
    table = np.zeros((32, 2, 4, 2, 4, 32))
    for low in range(4):
        table[:, 0, low, 0, low, :] = cos
        table[:, 0, low, 1, low, :] = -sin
        table[:, 1, low, 0, low, :] = sin
        table[:, 1, low, 1, low, :] = cos
    tabs["M1"] = table.reshape(256, 256) / GRID
    for name, sign in (("L2", 1.0), ("M2", -1.0)):
        table = np.zeros((2, 4, 32, 2, 4, 32))
        for slot in range(4):
            table[0, slot, :, 0, slot, :] = cos
            table[0, slot, :, 1, slot, :] = -sign * sin
            table[1, slot, :, 0, slot, :] = sign * sin
            table[1, slot, :, 1, slot, :] = cos
        tabs[name] = table.reshape(256, 256)
    return tabs


def make_constants():
    offsets, parts, at = {}, [], 0
    for name, table in make_tables().items():
        table = table.astype(np.float32)
        high = table.astype(ml_dtypes.bfloat16)
        low = (table - high.astype(np.float32)).astype(ml_dtypes.bfloat16)
        count = table.shape[0]
        offsets[name] = (at, count)
        parts += [high, low]
        at += 2 * count
    small = np.arange(128)
    short = np.arange(32)
    twist = np.zeros((96, 128))
    angle = 2 * np.pi / GRID * ((np.arange(1, 4)[:, None] * small[None, :]) % GRID)
    twist[0:3], twist[8:11] = np.cos(angle), np.sin(angle)
    angle = 2 * np.pi / GRID * ((short[:, None] * short[None, :]) % GRID)
    twist[16:48] = np.tile(np.cos(angle), (1, 4))
    twist[48:80] = np.tile(np.sin(angle), (1, 4))
    for slot in range(4):
        freq = 4 * small if slot == 0 else slot + 8 * small
        freq = np.where(freq < GRID // 2, freq, freq - GRID) * (8.0 / GRID)
        lanes = np.stack([freq.reshape(32, 4)] * 2, axis=1).reshape(256)
        twist[80 + slot], twist[88 + slot] = lanes[:128], lanes[128:]
    return offsets, np.concatenate(parts, 0), twist.astype(np.float32)


OFFSETS, TABLE, TWIST = make_constants()


def dot(left, right):
    return jnp.dot(left, right, preferred_element_type=jnp.float32)


def halves(value):
    high = value.astype(jnp.bfloat16)
    return high, (value - high.astype(jnp.float32)).astype(jnp.bfloat16)


def phi_triple(scaled):
    small = jnp.abs(scaled) < 0.5
    safe = jnp.where(small, jnp.ones_like(scaled), scaled)
    inverse = 1.0 / safe
    growth = jnp.exp(safe) - 1.0
    first_phi = growth * inverse
    second_phi = (first_phi - 1.0) * inverse
    series_one = jnp.zeros_like(scaled)
    series_two = jnp.zeros_like(scaled)
    for power in range(10, -1, -1):
        fact_one = float(math.factorial(power + 1))
        series_one = series_one * scaled + 1.0 / fact_one
        series_two = series_two * scaled + 1.0 / (fact_one * (power + 2))
    return (
        jnp.exp(scaled),
        jnp.where(small, series_one, first_phi),
        jnp.where(small, series_two, second_phi),
    )


def kernel(
    steps_ref, shift_ref, basis_hbm, grad_hbm, table_hbm, twist_hbm,
    out_ref, hess_ref,
    basis, grad, table, twist, counts,
    s1, s2, s3, s4, s5, s6, r1, r2, r3, r4, r5, r6,
    mine, sum_a, sum_b,
    local_sem, send_sem, recv_sem, ready,
):
    seg = lax.axis_index("seg")
    me = lax.axis_index("space")
    other = seg + 2 - 4 * (lax.rem(seg, 4) // 2)
    half, place = me // 16, lax.rem(me, 16)
    column_y, core = place // 2, lax.rem(place, 2)
    chip_x, chip_z = seg // 4, lax.rem(seg, 4) + 4 * half
    f32 = jnp.float32

    loads = [
        pltpu.make_async_copy(source, target, local_sem.at[at])
        for at, (source, target) in enumerate(
            ((basis_hbm, basis), (twist_hbm, twist), (table_hbm, table), (grad_hbm, grad))
        )
    ]
    for load in loads:
        load.start()

    before = lax.rem(seg + SEGS - 1, SEGS)
    before = before + 2 - 4 * (lax.rem(before, 4) // 2)
    after = lax.rem(other + 1, SEGS)

    barrier = pltpu.get_barrier_semaphore()

    def far_first(step, size):
        away = (step + 1) // 2
        return lax.rem(size + size // 2 + away * (1 - 2 * lax.rem(step, 2)), size)

    def peer_in_space(step):
        inner = lax.rem(step, 4)
        chip_y = lax.rem(column_y + far_first(step // 4, 8), 8)
        peer_core = lax.rem(core + 1 + lax.rem(inner, 2), 2)
        return 16 * (inner // 2) + 2 * chip_y + peer_core

    def peer_in_plane(step):
        peer_z = lax.rem(chip_z + far_first(step // 4, 8), 8)
        peer_x = lax.rem(chip_x + far_first(lax.rem(step, 4), 4), 4)
        return {"seg": 4 * peer_x + lax.rem(peer_z, 4), "space": 16 * (peer_z // 4) + place}

    def peer_in_column(step):
        chip_y = lax.rem(column_y + far_first(step // 2, 8), 8)
        peer_core = lax.rem(core + 1 + lax.rem(step, 2), 2)
        return {"space": 16 * half + 2 * chip_y + peer_core}

    def greet_space(step, carry):
        pl.semaphore_signal(
            barrier, inc=1, device_id={"seg": other, "space": peer_in_space(step)}, device_id_type=MESH
        )
        return carry

    def greet_plane(step, carry):
        pl.semaphore_signal(barrier, inc=1, device_id=peer_in_plane(step), device_id_type=MESH)
        return carry

    lax.fori_loop(0, SPACE, greet_space, 0)
    lax.fori_loop(0, PLANE - 1, greet_plane, 0)

    def const(name):
        at, count = OFFSETS[name]
        return table[at : at + count, :], table[at + count : at + 2 * count, :]

    def const_left(name, value):
        high, low = halves(value)
        table_high, table_low = const(name)
        both = dot(table_high, jnp.concatenate([high, low], axis=1))
        return both[:, :128] + both[:, 128:] + dot(table_low, high)

    def const_right(value, name):
        count = value.shape[0]
        high, low = halves(value)
        table_high, table_low = const(name)
        both = dot(jnp.concatenate([high, low], axis=0), table_high)
        return both[:count] + both[count:] + dot(high, table_low)

    def send(source, target, at, rows, to_seg):
        def step_to(step, carry):
            peer = peer_in_space(step)
            pltpu.make_async_remote_copy(
                src_ref=source.at[pl.ds(pl.multiple_of(peer * rows, 8), rows)],
                dst_ref=target.at[pl.ds(pl.multiple_of(me * rows, 8), rows)],
                send_sem=send_sem.at[at],
                recv_sem=recv_sem.at[at],
                device_id={"seg": to_seg, "space": peer},
                device_id_type=MESH,
            ).start()
            return carry

        lax.fori_loop(0, SPACE, step_to, 0)

    def arrival(source, target, at, rows):
        return pltpu.make_async_remote_copy(
            src_ref=source.at[pl.ds(0, rows)],
            dst_ref=target.at[pl.ds(0, rows)],
            send_sem=send_sem.at[at],
            recv_sem=recv_sem.at[at],
            device_id={"space": me},
            device_id_type=MESH,
        )

    def row_spectrum(field):
        group = [field[:, 128 * at : 128 * at + 128] for at in range(8)]
        plus = [group[at] + group[at + 4] for at in range(4)]
        minus = [group[at] - group[at + 4] for at in range(4)]
        zero = jnp.concatenate([plus[0] + plus[2], plus[1] + plus[3]], axis=1)
        inner = HALF * (minus[1] - minus[3])
        outer = HALF * (minus[1] + minus[3])
        pairs = (
            (minus[0] + inner, -(minus[2] + outer)),
            (plus[0] - plus[2], plus[3] - plus[1]),
            (minus[0] - inner, minus[2] - outer),
        )
        rest = []
        for at, (real, imag) in enumerate(pairs):
            cos, sin = twist[at : at + 1, :], twist[8 + at : 9 + at, :]
            rest.append(
                jnp.concatenate([real * cos + imag * sin, imag * cos - real * sin], axis=1)
            )
        return const_right(zero, "A0"), const_right(jnp.concatenate(rest, axis=0), "A1")

    def row_field(zero, rest):
        turned = []
        for at in range(3):
            real, imag = rest[32 * at : 32 * at + 32, :128], rest[32 * at : 32 * at + 32, 128:]
            cos, sin = twist[at : at + 1, :], twist[8 + at : 9 + at, :]
            turned.append((real * cos - imag * sin, real * sin + imag * cos))
        (re1, im1), (re2, im2), (re3, im3) = turned
        even, odd = zero[:, :128], zero[:, 128:]
        sums = (even + re2, odd - im2, even - re2, odd + im2)
        differences = (
            re1 + re3,
            HALF * ((re1 - im1) - (re3 + im3)),
            im3 - im1,
            HALF * ((re3 - im3) - (re1 + im1)),
        )
        pieces = [sums[at] + differences[at] for at in range(4)]
        pieces += [sums[at] - differences[at] for at in range(4)]
        return jnp.concatenate(pieces, axis=1)

    def rows_forward(field, target):
        zero, rest = row_spectrum(field)
        target[...] = jnp.concatenate([zero, rest], axis=0).T
        return zero, rest

    def rows_inverse(received):
        turned = received.T
        return row_field(const_right(turned[:32], "B0"), const_right(turned[32:], "B1"))

    def stacked(value):
        return jnp.concatenate([value] * 5, axis=0)

    lane = lax.broadcasted_iota(jnp.int32, (160, 128), 1)
    row = lax.broadcasted_iota(jnp.int32, (160, 128), 0)
    anchor = jnp.where((lane[:32] < 32) & (me == 0), 1.0, 0.0).astype(f32)

    def columns_forward(received):
        value = const_left("L1", received)
        real, imag = value[:160], value[160:]
        real = jnp.concatenate([real[:32] + anchor * imag[128:], real[32:]], axis=0)
        imag = jnp.concatenate([imag[:32] - anchor * value[128:160], imag[32:]], axis=0)
        cos, sin = stacked(twist[16:48, :]), stacked(twist[48:80, :])
        turned = jnp.concatenate([real * cos + imag * sin, imag * cos - real * sin], axis=1)
        value = const_right(turned, "L2")
        return value[:, :128], value[:, 128:]

    def columns_inverse(real, imag):
        value = const_right(jnp.concatenate([real, imag], axis=1), "M2")
        real, imag = value[:, :128], value[:, 128:]
        cos, sin = stacked(twist[16:48, :]), stacked(twist[48:80, :])
        real, imag = real * cos - imag * sin, real * sin + imag * cos
        value = jnp.concatenate(
            [real[:32] - anchor * imag[128:], real[32:128], imag[:32] + anchor * real[128:], imag[32:128]],
            axis=0,
        )
        return const_left("M1", value)

    loads[0].wait()
    loads[1].wait()
    loads[2].wait()
    start = basis[KRYLOV - 1].astype(f32)
    zero, rest = rows_forward(start, s1)
    pl.semaphore_wait(barrier, SPACE + PLANE - 1)
    counts[0] = jnp.full((1, 128), steps_ref[0], jnp.int32)
    count_copy = pltpu.make_async_remote_copy(
        src_ref=counts.at[0],
        dst_ref=counts.at[1],
        send_sem=send_sem.at[8],
        recv_sem=recv_sem.at[8],
        device_id={"seg": other},
        device_id_type=MESH,
    )
    count_copy.start()
    send(s1, r1, 0, 8, other)

    waves = [
        jnp.concatenate([twist[80 + at : 81 + at, :], twist[88 + at : 89 + at, :]], axis=1)
        for at in range(4)
    ]
    lifted = jnp.concatenate([rest[32 * at : 32 * at + 32] * waves[at + 1] for at in range(3)], axis=0)
    grad_y = row_field(const_right(zero * waves[0], "D0"), const_right(lifted, "D1"))

    slot = lane // 32
    low = row // 32
    freq_x = row % 32 + 32 * (lane % 32)
    base = 4 * me + low
    freq_y = jnp.where(low == 4, GRID // 2, jnp.where(slot == 0, 4 * base, slot + 8 * base))
    signed_x = jnp.where(freq_x < GRID // 2, freq_x, freq_x - GRID)
    signed_y = jnp.where(freq_y < GRID // 2, freq_y, freq_y - GRID)
    wave_x = signed_x.astype(f32) * (8.0 / GRID)
    wave_y = signed_y.astype(f32) * (8.0 / GRID)
    deriv_x = jnp.where(signed_x == -(GRID // 2), 0.0, wave_x)
    deriv_y = jnp.where(signed_y == -(GRID // 2), 0.0, wave_y)
    squared = wave_x * wave_x + wave_y * wave_y
    count_copy.wait_recv()
    step_size = 0.01 * counts[1].astype(f32)
    decay, phi_one, phi_two = phi_triple((squared - squared * squared) * step_size)
    phi_one = step_size * phi_one
    phi_two = step_size * phi_two

    done = arrival(s1, r1, 0, 256)
    done.wait_recv()
    state_re, state_im = columns_forward(r1[...])

    s2[...] = columns_inverse(-deriv_x * state_im, deriv_x * state_re)
    send(s2, r2, 1, 8, other)
    loads[3].wait()
    part_y = grad[1].astype(f32) * grad_y
    part_x = -grad[0].astype(f32)
    arrival(s2, r2, 1, 256).wait_recv()
    pl.semaphore_signal(ready, inc=1, device_id={"seg": before}, device_id_type=MESH)
    term = part_x * rows_inverse(r2[...]) - part_y

    rows_forward(term, s3)
    send(s3, r3, 2, 8, other)
    flat = basis[...].reshape(KRYLOV * ROWS, GRID)
    gram = lax.dot_general(flat, flat, (((1,), (1,)), ((), ())), preferred_element_type=f32)
    gram_row = lax.broadcasted_iota(jnp.int32, (256, 256), 0)
    gram_lane = lax.broadcasted_iota(jnp.int32, (256, 256), 1)
    gram = jnp.where(gram_row % 32 == gram_lane % 32, gram, 0.0)
    gram = jnp.concatenate(
        [jnp.sum(gram[32 * at : 32 * at + 32], axis=0, keepdims=True) for at in range(8)], axis=0
    )
    spot_row = lax.broadcasted_iota(jnp.int32, (8, 128), 0)
    spot_lane = lax.broadcasted_iota(jnp.int32, (8, 128), 1)
    gram_sums = jnp.zeros((8, 128), f32)
    for at in range(8):
        part = jnp.sum(jnp.where(gram_lane[:8] // 32 == at, gram, 0.0), axis=1, keepdims=True)
        gram_sums = gram_sums + jnp.where(spot_lane == 16 + 8 * spot_row + at, part, 0.0)
    gram_sums = jnp.sum(gram_sums, axis=0, keepdims=True)
    arrival(s3, r3, 2, 256).wait_recv()
    term_re, term_im = columns_forward(r3[...])
    middle_re = decay * state_re + phi_one * term_re
    middle_im = decay * state_im + phi_one * term_im

    toward_x = columns_inverse(-deriv_x * middle_im, deriv_x * middle_re)
    toward_y = columns_inverse(-deriv_y * middle_im, deriv_y * middle_re)
    for peer in range(SPACE):
        s4[16 * peer : 16 * peer + 8, :] = toward_x[8 * peer : 8 * peer + 8]
        s4[16 * peer + 8 : 16 * peer + 16, :] = toward_y[8 * peer : 8 * peer + 8]
    send(s4, r4, 3, 16, other)
    offset = (freq_x * shift_ref[0] + freq_y * shift_ref[1]) & (GRID - 1)
    angle = (2.0 * math.pi / GRID) * offset.astype(f32)
    is_last = other == SEGS - 1
    cosine = jnp.where(is_last, jnp.cos(angle), 1.0)
    sine = jnp.where(is_last, jnp.sin(angle), 0.0)
    arrival(s4, r4, 3, 512).wait_recv()
    got_x = jnp.concatenate([r4[16 * peer : 16 * peer + 8, :] for peer in range(SPACE)], axis=0)
    got_y = jnp.concatenate([r4[16 * peer + 8 : 16 * peer + 16, :] for peer in range(SPACE)], axis=0)
    term = -(grad[2].astype(f32) * rows_inverse(got_x) + grad[3].astype(f32) * rows_inverse(got_y))

    rows_forward(term, s5)
    send(s5, r5, 4, 8, other)
    kept_re = middle_re - phi_two * term_re
    kept_im = middle_im - phi_two * term_im
    arrival(s5, r5, 4, 256).wait_recv()
    term_re, term_im = columns_forward(r5[...])
    state_re = kept_re + phi_two * term_re
    state_im = kept_im + phi_two * term_im

    s6[...] = columns_inverse(cosine * state_re + sine * state_im, cosine * state_im - sine * state_re)
    pl.semaphore_wait(ready, 1)
    send(s6, r6, 5, 8, after)
    arrival(s6, r6, 5, 256).wait_recv()
    wrapped = rows_inverse(r6[...]) - start

    def folded(value):
        total = value[:, :128]
        for at in range(1, 8):
            total = total + value[:, 128 * at : 128 * at + 128]
        return jnp.sum(total, axis=0, keepdims=True)

    lines = [folded(wrapped * basis[at].astype(f32)) for at in range(KRYLOV)]
    lines.append(folded(wrapped * wrapped))
    lines.append(jnp.zeros((7, 128), f32))
    sums = jnp.sum(jnp.concatenate(lines, axis=0), axis=1, keepdims=True)
    spot_row = lax.broadcasted_iota(jnp.int32, (16, 128), 0)
    spot_lane = lax.broadcasted_iota(jnp.int32, (16, 128), 1)
    line = jnp.sum(jnp.where(spot_row == spot_lane, sums, 0.0), axis=0, keepdims=True) + gram_sums

    def spread(target, peer_of, own, count, at):
        target[own] = mine[at]

        def step_to(step, carry):
            pltpu.make_async_remote_copy(
                src_ref=mine.at[at],
                dst_ref=target.at[own],
                send_sem=send_sem.at[6 + at],
                recv_sem=recv_sem.at[6 + at],
                device_id=peer_of(step),
                device_id_type=MESH,
            ).start()
            return carry

        lax.fori_loop(0, count - 1, step_to, 0)
        done = pltpu.make_async_remote_copy(
            src_ref=target.at[pl.ds(0, count - 1)],
            dst_ref=target.at[pl.ds(0, count - 1)],
            send_sem=send_sem.at[6 + at],
            recv_sem=recv_sem.at[6 + at],
            device_id={"seg": other},
            device_id_type=MESH,
        )
        done.wait_recv()
        return done, jnp.sum(target[...], axis=0)

    mine[0] = line
    sent_a, line = spread(sum_a, peer_in_column, place, COLUMN, 0)
    mine[1] = line
    sent_b, line = spread(sum_b, peer_in_plane, 8 * chip_x + chip_z, PLANE, 1)
    line = line * (1.0 / (SEGS * GRID * GRID))

    lanes = lax.broadcasted_iota(jnp.int32, (1, 128), 1)

    def lane_of(at):
        return jnp.sum(jnp.where(lanes == at, line, 0.0), axis=1, keepdims=True)

    coeffs = [lane_of(at) for at in range(KRYLOV)]
    norm_sq = lane_of(KRYLOV)
    left = jnp.zeros((1, 128), f32)
    right = jnp.zeros((1, 128), f32)
    for at in range(KRYLOV):
        left = left + jnp.where((lanes >= 16 + 8 * at) & (lanes < 24 + 8 * at), coeffs[at], 0.0)
        right = right + jnp.where((lanes >= 16) & (lanes % 8 == at) & (lanes < 80), coeffs[at], 0.0)
        norm_sq = norm_sq - 2.0 * coeffs[at] * coeffs[at]
    norm_sq = norm_sq + jnp.sum(left * right * line, axis=1, keepdims=True)
    norm = jnp.sqrt(norm_sq)
    hess_ref[...] = jnp.where(lanes == KRYLOV, norm, line)
    inverse = 1.0 / norm
    remainder = wrapped
    for at in range(KRYLOV):
        remainder = remainder - coeffs[at] * basis[at].astype(f32)
    out_ref[0] = remainder * inverse

    for source, at, rows in ((s1, 0, 256), (s2, 1, 256), (s3, 2, 256), (s4, 3, 512), (s5, 4, 256), (s6, 5, 256)):
        arrival(source, source, at, rows).wait_send()
    sent_a.wait_send()
    sent_b.wait_send()
    count_copy.wait_send()


def per_device(basis, base_grad, step_counts, shift):
    any_space = pl.BlockSpec(memory_space=pl.ANY)
    scalars = pl.BlockSpec(memory_space=pltpu.SMEM)
    f32, bf16 = jnp.float32, jnp.bfloat16
    tile = pltpu.VMEM((256, 128), f32)
    wide = pltpu.VMEM((512, 128), f32)
    new_vector, line = pl.pallas_call(
        kernel,
        out_shape=(
            jax.ShapeDtypeStruct((1, ROWS, GRID), f32),
            jax.ShapeDtypeStruct((1, 128), f32),
        ),
        in_specs=[scalars, scalars] + [any_space] * 4,
        out_specs=(pl.BlockSpec(memory_space=pltpu.VMEM),) * 2,
        scratch_shapes=[
            pltpu.VMEM((KRYLOV, ROWS, GRID), bf16),
            pltpu.VMEM((4, ROWS, GRID), bf16),
            pltpu.VMEM(TABLE.shape, bf16),
            pltpu.VMEM(TWIST.shape, f32),
            pltpu.VMEM((2, 1, 128), jnp.int32),
            tile, tile, tile, wide, tile, tile,
            tile, tile, tile, wide, tile, tile,
            pltpu.VMEM((2, 1, 128), f32),
            pltpu.VMEM((COLUMN, 1, 128), f32),
            pltpu.VMEM((PLANE, 1, 128), f32),
            pltpu.SemaphoreType.DMA((4,)),
            pltpu.SemaphoreType.DMA((9,)),
            pltpu.SemaphoreType.DMA((9,)),
            pltpu.SemaphoreType.REGULAR,
        ],
        compiler_params=pltpu.CompilerParams(
            collective_id=0, has_side_effects=True, vmem_limit_bytes=62 * 1024 * 1024
        ),
    )(
        step_counts,
        shift,
        basis[0],
        base_grad.reshape(4, ROWS, GRID),
        jnp.asarray(TABLE),
        jnp.asarray(TWIST),
    )
    return new_vector, line[0, : KRYLOV + 1]


def solution(mesh):
    in_specs = (P("seg", None, "space", None), P("seg", None, None, "space", None), P("seg"), P())
    out_specs = (P("seg", "space", None), P())
    return jax.shard_map(
        per_device, mesh=mesh, in_specs=in_specs, out_specs=out_specs, check_vma=False
    )
```

```python
import math

import jax
import jax.numpy as jnp
import ml_dtypes
import numpy as np
from jax import lax
from jax.experimental import pallas as pl
from jax.experimental.pallas import tpu as pltpu
from jax.sharding import PartitionSpec as P

MESH = pl.DeviceIdType.MESH
GRID = 1024
SPACE = 32
SEGS = 16
KRYLOV = 8
PLANE = 32
COLUMN = 16
ROWS = GRID // SPACE
HALF = math.sqrt(0.5)


def make_tables():
    tabs = {}
    small = np.arange(128)
    full = np.arange(256)
    short = np.arange(32)

    def by_owner(real, imag):
        parts = [part.reshape(part.shape[0], 32, 4) for part in (real, imag)]
        return np.stack(parts, axis=2).reshape(real.shape[0], 256)

    def owner_rows(real, imag):
        parts = [part.reshape(32, 4, -1) for part in (real, imag)]
        return np.stack(parts, axis=1).reshape(256, -1)

    def swapped(table):
        parts = table.reshape(32, 2, 4, 256)
        return np.stack([parts[:, 1], -parts[:, 0]], axis=1).reshape(256, 256)

    angle = 2 * np.pi / 256 * ((full[:, None] * small[None, :]) % 256)
    real, imag = np.cos(angle), -np.sin(angle)
    imag[:, 0] = (-1.0) ** full
    tabs["A0"] = by_owner(real, imag)
    real, imag = 2 * np.cos(angle.T), -2 * np.sin(angle.T)
    real[0], imag[0] = 1.0, (-1.0) ** full
    tabs["B0"] = owner_rows(real, imag) / GRID
    angle = 2 * np.pi / 128 * ((small[:, None] * small[None, :]) % 128)
    cos, sin = np.cos(angle), np.sin(angle)
    tabs["A1"] = np.concatenate([by_owner(cos, -sin), by_owner(sin, cos)], 0)
    real = np.concatenate([cos, sin], 1)
    imag = np.concatenate([-sin, cos], 1)
    tabs["B1"] = owner_rows(real, imag) * 2 / GRID
    tabs["D0"] = swapped(tabs["B0"])
    tabs["D1"] = swapped(tabs["B1"])
    angle = 2 * np.pi / 32 * ((short[:, None] * short[None, :]) % 32)
    cos, sin = np.cos(angle), np.sin(angle)
    table = np.zeros((2, 5, 32, 32, 2, 4))
    for low in range(4):
        table[0, low, :, :, 0, low] = cos
        table[0, low, :, :, 1, low] = sin
        table[1, low, :, :, 0, low] = -sin
        table[1, low, :, :, 1, low] = cos
    table[0, 4, :, :, 1, 0] = cos
    table[1, 4, :, :, 1, 0] = -sin
    tabs["L1"] = table.reshape(320, 256)
    table = np.zeros((32, 2, 4, 2, 4, 32))
    for low in range(4):
        table[:, 0, low, 0, low, :] = cos
        table[:, 0, low, 1, low, :] = -sin
        table[:, 1, low, 0, low, :] = sin
        table[:, 1, low, 1, low, :] = cos
    tabs["M1"] = table.reshape(256, 256) / GRID
    for name, sign in (("L2", 1.0), ("M2", -1.0)):
        table = np.zeros((2, 4, 32, 2, 4, 32))
        for slot in range(4):
            table[0, slot, :, 0, slot, :] = cos
            table[0, slot, :, 1, slot, :] = -sign * sin
            table[1, slot, :, 0, slot, :] = sign * sin
            table[1, slot, :, 1, slot, :] = cos
        tabs[name] = table.reshape(256, 256)
    return tabs


def make_constants():
    offsets, parts, at = {}, [], 0
    for name, table in make_tables().items():
        table = table.astype(np.float32)
        high = table.astype(ml_dtypes.bfloat16)
        low = (table - high.astype(np.float32)).astype(ml_dtypes.bfloat16)
        count = table.shape[0]
        offsets[name] = (at, count)
        parts += [high, low]
        at += 2 * count
    small = np.arange(128)
    short = np.arange(32)
    twist = np.zeros((1024, 128))
    angle = 2 * np.pi / GRID * ((np.arange(1, 4)[:, None] * small[None, :]) % GRID)
    twist[0:3], twist[8:11] = np.cos(angle), np.sin(angle)
    angle = 2 * np.pi / GRID * ((short[:, None] * short[None, :]) % GRID)
    twist[16:48] = np.tile(np.cos(angle), (1, 4))
    twist[48:80] = np.tile(np.sin(angle), (1, 4))
    for slot in range(4):
        freq = 4 * small if slot == 0 else slot + 8 * small
        freq = np.where(freq < GRID // 2, freq, freq - GRID) * (8.0 / GRID)
        lanes = np.stack([freq.reshape(32, 4)] * 2, axis=1).reshape(256)
        twist[80 + slot], twist[88 + slot] = lanes[:128], lanes[128:]
    return offsets, np.concatenate(parts, 0), twist.astype(np.float32)


OFFSETS, TABLE, TWIST = make_constants()


def dot(left, right):
    return jnp.dot(left, right, preferred_element_type=jnp.float32)


def halves(value):
    high = value.astype(jnp.bfloat16)
    return high, (value - high.astype(jnp.float32)).astype(jnp.bfloat16)


def phi_triple(scaled):
    small = jnp.abs(scaled) < 0.5
    safe = jnp.where(small, jnp.ones_like(scaled), scaled)
    inverse = 1.0 / safe
    growth = jnp.exp(safe) - 1.0
    first_phi = growth * inverse
    second_phi = (first_phi - 1.0) * inverse
    series_one = jnp.zeros_like(scaled)
    series_two = jnp.zeros_like(scaled)
    for power in range(10, -1, -1):
        fact_one = float(math.factorial(power + 1))
        series_one = series_one * scaled + 1.0 / fact_one
        series_two = series_two * scaled + 1.0 / (fact_one * (power + 2))
    return (
        jnp.exp(scaled),
        jnp.where(small, series_one, first_phi),
        jnp.where(small, series_two, second_phi),
    )


def kernel(
    steps_ref, shift_ref, basis_hbm, grad_hbm, table_hbm, twist_hbm,
    out_ref, hess_ref,
    basis, grad, table, twist, counts,
    s1, s2, s3, s5, s6, r1, r2, r3, r5, r6,
    pairs_out, pairs_in, spectra,
    mine, sum_a, sum_b,
    local_sem, send_sem, recv_sem, ready,
):
    seg = lax.axis_index("seg")
    me = lax.axis_index("space")
    other = seg + 2 - 4 * (lax.rem(seg, 4) // 2)
    half, place = me // 16, lax.rem(me, 16)
    column_y, core = place // 2, lax.rem(place, 2)
    chip_x, chip_z = seg // 4, lax.rem(seg, 4) + 4 * half
    f32 = jnp.float32

    loads = [
        pltpu.make_async_copy(source, target, local_sem.at[at])
        for at, (source, target) in enumerate(
            ((basis_hbm, basis), (twist_hbm.at[pl.ds(0, 96)], twist), (table_hbm, table), (grad_hbm, grad))
        )
    ]
    for load in loads:
        load.start()

    before = lax.rem(seg + SEGS - 1, SEGS)
    before = before + 2 - 4 * (lax.rem(before, 4) // 2)
    after = lax.rem(other + 1, SEGS)

    barrier = pltpu.get_barrier_semaphore()

    def far_first(step, size):
        away = (step + 1) // 2
        return lax.rem(size + size // 2 + away * (1 - 2 * lax.rem(step, 2)), size)

    def peer_in_space(step):
        inner = lax.rem(step, 4)
        chip_y = lax.rem(column_y + far_first(step // 4, 8), 8)
        peer_core = lax.rem(core + 1 + lax.rem(inner, 2), 2)
        return 16 * (inner // 2) + 2 * chip_y + peer_core

    def peer_in_plane(step):
        peer_z = lax.rem(chip_z + far_first(step // 4, 8), 8)
        peer_x = lax.rem(chip_x + far_first(lax.rem(step, 4), 4), 4)
        return {"seg": 4 * peer_x + lax.rem(peer_z, 4), "space": 16 * (peer_z // 4) + place}

    def peer_in_column(step):
        chip_y = lax.rem(column_y + far_first(step // 2, 8), 8)
        peer_core = lax.rem(core + 1 + lax.rem(step, 2), 2)
        return {"space": 16 * half + 2 * chip_y + peer_core}

    def greet_space(step, carry):
        pl.semaphore_signal(
            barrier, inc=1, device_id={"seg": other, "space": peer_in_space(step)}, device_id_type=MESH
        )
        return carry

    def greet_plane(step, carry):
        pl.semaphore_signal(barrier, inc=1, device_id=peer_in_plane(step), device_id_type=MESH)
        return carry

    lax.fori_loop(0, SPACE, greet_space, 0)
    lax.fori_loop(0, PLANE - 1, greet_plane, 0)

    def const(name):
        at, count = OFFSETS[name]
        return table[at : at + count, :], table[at + count : at + 2 * count, :]

    def const_left(name, value):
        high, low = halves(value)
        table_high, table_low = const(name)
        both = dot(table_high, jnp.concatenate([high, low], axis=1))
        return both[:, :128] + both[:, 128:] + dot(table_low, high)

    def const_right(value, name):
        count = value.shape[0]
        high, low = halves(value)
        table_high, table_low = const(name)
        both = dot(jnp.concatenate([high, low], axis=0), table_high)
        return both[:count] + both[count:] + dot(high, table_low)

    def send(source, target, at, rows, to_seg):
        def step_to(step, carry):
            peer = peer_in_space(step)
            pltpu.make_async_remote_copy(
                src_ref=source.at[pl.ds(pl.multiple_of(peer * rows, 8), rows)],
                dst_ref=target.at[pl.ds(pl.multiple_of(me * rows, 8), rows)],
                send_sem=send_sem.at[at],
                recv_sem=recv_sem.at[at],
                device_id={"seg": to_seg, "space": peer},
                device_id_type=MESH,
            ).start()
            return carry

        lax.fori_loop(0, SPACE, step_to, 0)

    def arrival(source, target, at, rows):
        return pltpu.make_async_remote_copy(
            src_ref=source.at[pl.ds(0, rows)],
            dst_ref=target.at[pl.ds(0, rows)],
            send_sem=send_sem.at[at],
            recv_sem=recv_sem.at[at],
            device_id={"space": me},
            device_id_type=MESH,
        )

    def coded(value):
        top = jnp.maximum(jnp.max(jnp.abs(value), axis=0, keepdims=True), 1e-30)
        level = jnp.ceil(256.0 * jnp.log2(top)).astype(jnp.int32) + 1
        scale = jnp.exp2(15.0 - level.astype(f32) * (1.0 / 256.0))
        return jnp.floor(value * scale + 0.5).astype(jnp.int32), level

    def joined(high, low):
        return (high << 16) | (low & 0xFFFF)

    def parted(word):
        return word >> 16, (word << 16) >> 16

    def send_pair(first, second, at, to_seg):
        first_code, first_level = coded(first)
        second_code, second_level = coded(second)
        pairs_out[at, :, 0:8, :] = joined(first_code, second_code).reshape(SPACE, 8, 128)
        level = joined(first_level, second_level)
        pairs_out[at, :, 8:9, :] = jnp.broadcast_to(level.reshape(1, 1, 128), (SPACE, 1, 128))

        def step_to(step, carry):
            peer = peer_in_space(step)
            pltpu.make_async_remote_copy(
                src_ref=pairs_out.at[at, peer],
                dst_ref=pairs_in.at[at, me],
                send_sem=send_sem.at[9 + at],
                recv_sem=recv_sem.at[9 + at],
                device_id={"seg": to_seg, "space": peer},
                device_id_type=MESH,
            ).start()
            return carry

        lax.fori_loop(0, SPACE, step_to, 0)

    def pair_done(at):
        return pltpu.make_async_remote_copy(
            src_ref=pairs_out.at[at],
            dst_ref=pairs_in.at[at],
            send_sem=send_sem.at[9 + at],
            recv_sem=recv_sem.at[9 + at],
            device_id={"space": me},
            device_id_type=MESH,
        )

    def received_pair(at):
        codes = parted(pairs_in[at, :, 0:8, :])
        levels = parted(pairs_in[at, :, 8:9, :])
        return [
            (code.astype(f32) * jnp.exp2(level.astype(f32) * (1.0 / 256.0) - 15.0)).reshape(256, 128)
            for code, level in zip(codes, levels)
        ]

    def basis_spectra(at):
        for index in (2 * at, 2 * at + 1):
            if index == KRYLOV - 1:
                spectra[index] = weight * s1[...]
            else:
                zero, rest = row_spectrum(basis[index].astype(f32))
                spectra[index] = weight * jnp.concatenate([zero, rest], axis=0).T

    def row_spectrum(field):
        group = [field[:, 128 * at : 128 * at + 128] for at in range(8)]
        plus = [group[at] + group[at + 4] for at in range(4)]
        minus = [group[at] - group[at + 4] for at in range(4)]
        zero = jnp.concatenate([plus[0] + plus[2], plus[1] + plus[3]], axis=1)
        inner = HALF * (minus[1] - minus[3])
        outer = HALF * (minus[1] + minus[3])
        pairs = (
            (minus[0] + inner, -(minus[2] + outer)),
            (plus[0] - plus[2], plus[3] - plus[1]),
            (minus[0] - inner, minus[2] - outer),
        )
        rest = []
        for at, (real, imag) in enumerate(pairs):
            cos, sin = twist[at : at + 1, :], twist[8 + at : 9 + at, :]
            rest.append(
                jnp.concatenate([real * cos + imag * sin, imag * cos - real * sin], axis=1)
            )
        return const_right(zero, "A0"), const_right(jnp.concatenate(rest, axis=0), "A1")

    def row_field(zero, rest):
        turned = []
        for at in range(3):
            real, imag = rest[32 * at : 32 * at + 32, :128], rest[32 * at : 32 * at + 32, 128:]
            cos, sin = twist[at : at + 1, :], twist[8 + at : 9 + at, :]
            turned.append((real * cos - imag * sin, real * sin + imag * cos))
        (re1, im1), (re2, im2), (re3, im3) = turned
        even, odd = zero[:, :128], zero[:, 128:]
        sums = (even + re2, odd - im2, even - re2, odd + im2)
        differences = (
            re1 + re3,
            HALF * ((re1 - im1) - (re3 + im3)),
            im3 - im1,
            HALF * ((re3 - im3) - (re1 + im1)),
        )
        pieces = [sums[at] + differences[at] for at in range(4)]
        pieces += [sums[at] - differences[at] for at in range(4)]
        return jnp.concatenate(pieces, axis=1)

    def rows_forward(field, target):
        zero, rest = row_spectrum(field)
        target[...] = jnp.concatenate([zero, rest], axis=0).T
        return zero, rest

    def rows_inverse(received):
        turned = received.T
        return row_field(const_right(turned[:32], "B0"), const_right(turned[32:], "B1"))

    def stacked(value):
        return jnp.concatenate([value] * 5, axis=0)

    lane = lax.broadcasted_iota(jnp.int32, (160, 128), 1)
    row = lax.broadcasted_iota(jnp.int32, (160, 128), 0)
    anchor = jnp.where((lane[:32] < 32) & (me == 0), 1.0, 0.0).astype(f32)

    def columns_forward(received):
        value = const_left("L1", received)
        real, imag = value[:160], value[160:]
        real = jnp.concatenate([real[:32] + anchor * imag[128:], real[32:]], axis=0)
        imag = jnp.concatenate([imag[:32] - anchor * value[128:160], imag[32:]], axis=0)
        cos, sin = stacked(twist[16:48, :]), stacked(twist[48:80, :])
        turned = jnp.concatenate([real * cos + imag * sin, imag * cos - real * sin], axis=1)
        value = const_right(turned, "L2")
        return value[:, :128], value[:, 128:]

    def columns_inverse(real, imag):
        value = const_right(jnp.concatenate([real, imag], axis=1), "M2")
        real, imag = value[:, :128], value[:, 128:]
        cos, sin = stacked(twist[16:48, :]), stacked(twist[48:80, :])
        real, imag = real * cos - imag * sin, real * sin + imag * cos
        value = jnp.concatenate(
            [real[:32] - anchor * imag[128:], real[32:128], imag[:32] + anchor * real[128:], imag[32:128]],
            axis=0,
        )
        return const_left("M1", value)

    pair_row = lax.broadcasted_iota(jnp.int32, (256, 128), 0)
    pair_lane = lax.broadcasted_iota(jnp.int32, (256, 128), 1)
    alone = (pair_row < 8) & (pair_row % 4 == 0) & (pair_lane < 32)
    weight = jnp.where(alone, 1.0 / GRID, 2.0 / GRID).astype(f32)

    loads[0].wait()
    loads[1].wait()
    loads[2].wait()
    start = basis[KRYLOV - 1].astype(f32)
    zero, rest = rows_forward(start, s1)
    pl.semaphore_wait(barrier, SPACE + PLANE - 1)
    counts[0] = jnp.full((1, 128), steps_ref[0], jnp.int32)
    count_copy = pltpu.make_async_remote_copy(
        src_ref=counts.at[0],
        dst_ref=counts.at[1],
        send_sem=send_sem.at[8],
        recv_sem=recv_sem.at[8],
        device_id={"seg": other},
        device_id_type=MESH,
    )
    count_copy.start()
    send(s1, r1, 0, 8, other)
    basis_spectra(0)

    waves = [
        jnp.concatenate([twist[80 + at : 81 + at, :], twist[88 + at : 89 + at, :]], axis=1)
        for at in range(4)
    ]
    lifted = jnp.concatenate([rest[32 * at : 32 * at + 32] * waves[at + 1] for at in range(3)], axis=0)
    grad_y = row_field(const_right(zero * waves[0], "D0"), const_right(lifted, "D1"))

    slot = lane // 32
    low = row // 32
    freq_x = row % 32 + 32 * (lane % 32)
    base = 4 * me + low
    freq_y = jnp.where(low == 4, GRID // 2, jnp.where(slot == 0, 4 * base, slot + 8 * base))
    signed_x = jnp.where(freq_x < GRID // 2, freq_x, freq_x - GRID)
    signed_y = jnp.where(freq_y < GRID // 2, freq_y, freq_y - GRID)
    wave_x = signed_x.astype(f32) * (8.0 / GRID)
    wave_y = signed_y.astype(f32) * (8.0 / GRID)
    deriv_x = jnp.where(signed_x == -(GRID // 2), 0.0, wave_x)
    deriv_y = jnp.where(signed_y == -(GRID // 2), 0.0, wave_y)
    squared = wave_x * wave_x + wave_y * wave_y
    count_copy.wait_recv()
    step_size = 0.01 * counts[1].astype(f32)
    decay, phi_one, phi_two = phi_triple((squared - squared * squared) * step_size)
    phi_one = step_size * phi_one
    phi_two = step_size * phi_two

    done = arrival(s1, r1, 0, 256)
    done.wait_recv()
    state_re, state_im = columns_forward(r1[...])

    s2[...] = columns_inverse(-deriv_x * state_im, deriv_x * state_re)
    send(s2, r2, 1, 8, other)
    basis_spectra(1)
    loads[3].wait()
    part_y = grad[1].astype(f32) * grad_y
    part_x = -grad[0].astype(f32)
    arrival(s2, r2, 1, 256).wait_recv()
    pl.semaphore_signal(ready, inc=1, device_id={"seg": before}, device_id_type=MESH)
    term = part_x * rows_inverse(r2[...]) - part_y

    rows_forward(term, s3)
    send(s3, r3, 2, 8, other)
    basis_spectra(2)
    flat = basis[...].reshape(KRYLOV * ROWS, GRID)
    gram = lax.dot_general(flat, flat, (((1,), (1,)), ((), ())), preferred_element_type=f32)
    gram_row = lax.broadcasted_iota(jnp.int32, (256, 256), 0)
    gram_lane = lax.broadcasted_iota(jnp.int32, (256, 256), 1)
    gram = jnp.where(gram_row % 32 == gram_lane % 32, gram, 0.0)
    gram = jnp.concatenate(
        [jnp.sum(gram[32 * at : 32 * at + 32], axis=0, keepdims=True) for at in range(8)], axis=0
    )
    spot_row = lax.broadcasted_iota(jnp.int32, (8, 128), 0)
    spot_lane = lax.broadcasted_iota(jnp.int32, (8, 128), 1)
    gram_sums = jnp.zeros((8, 128), f32)
    for at in range(8):
        part = jnp.sum(jnp.where(gram_lane[:8] // 32 == at, gram, 0.0), axis=1, keepdims=True)
        gram_sums = gram_sums + jnp.where(spot_lane == 16 + 8 * spot_row + at, part, 0.0)
    gram_sums = jnp.sum(gram_sums, axis=0, keepdims=True)
    arrival(s3, r3, 2, 256).wait_recv()
    term_re, term_im = columns_forward(r3[...])
    middle_re = decay * state_re + phi_one * term_re
    middle_im = decay * state_im + phi_one * term_im

    toward_x = columns_inverse(-deriv_x * middle_im, deriv_x * middle_re)
    toward_y = columns_inverse(-deriv_y * middle_im, deriv_y * middle_re)
    send_pair(toward_x, toward_y, 0, other)
    basis_spectra(3)
    offset = (freq_x * shift_ref[0] + freq_y * shift_ref[1]) & (GRID - 1)
    angle = (2.0 * math.pi / GRID) * offset.astype(f32)
    is_last = other == SEGS - 1
    cosine = jnp.where(is_last, jnp.cos(angle), 1.0)
    sine = jnp.where(is_last, jnp.sin(angle), 0.0)
    pair_done(0).wait_recv()
    got_x, got_y = received_pair(0)
    term = -(grad[2].astype(f32) * rows_inverse(got_x) + grad[3].astype(f32) * rows_inverse(got_y))

    rows_forward(term, s5)
    send(s5, r5, 4, 8, other)
    kept_re = middle_re - phi_two * term_re
    kept_im = middle_im - phi_two * term_im
    arrival(s5, r5, 4, 256).wait_recv()
    term_re, term_im = columns_forward(r5[...])
    state_re = kept_re + phi_two * term_re
    state_im = kept_im + phi_two * term_im

    s6[...] = columns_inverse(cosine * state_re + sine * state_im, cosine * state_im - sine * state_re)
    pl.semaphore_wait(ready, 1)
    send(s6, r6, 5, 8, after)
    arrival(s6, r6, 5, 256).wait_recv()
    flow = r6[...]

    def folded(value):
        total = value[:8]
        for at in range(1, 32):
            total = total + value[8 * at : 8 * at + 8]
        return jnp.sum(total, axis=0, keepdims=True)

    lines = [folded(flow * spectra[at]) for at in range(KRYLOV)]
    lines.append(folded(flow * flow * weight))
    lines.append(jnp.zeros((7, 128), f32))
    sums = jnp.sum(jnp.concatenate(lines, axis=0), axis=1, keepdims=True)
    spot_row = lax.broadcasted_iota(jnp.int32, (16, 128), 0)
    spot_lane = lax.broadcasted_iota(jnp.int32, (16, 128), 1)
    line = jnp.sum(jnp.where(spot_row == spot_lane, sums, 0.0), axis=0, keepdims=True) + gram_sums

    def spread(target, peer_of, own, count, at):
        target[own] = mine[at]

        def step_to(step, carry):
            pltpu.make_async_remote_copy(
                src_ref=mine.at[at],
                dst_ref=target.at[own],
                send_sem=send_sem.at[6 + at],
                recv_sem=recv_sem.at[6 + at],
                device_id=peer_of(step),
                device_id_type=MESH,
            ).start()
            return carry

        lax.fori_loop(0, count - 1, step_to, 0)
        return pltpu.make_async_remote_copy(
            src_ref=target.at[pl.ds(0, count - 1)],
            dst_ref=target.at[pl.ds(0, count - 1)],
            send_sem=send_sem.at[6 + at],
            recv_sem=recv_sem.at[6 + at],
            device_id={"seg": other},
            device_id_type=MESH,
        )

    mine[0] = line
    sent_a = spread(sum_a, peer_in_column, place, COLUMN, 0)
    wrapped = rows_inverse(flow) - start
    sent_a.wait_recv()
    mine[1] = jnp.sum(sum_a[...], axis=0)
    sent_b = spread(sum_b, peer_in_plane, 8 * chip_x + chip_z, PLANE, 1)
    sent_b.wait_recv()
    line = jnp.sum(sum_b[...], axis=0) * (1.0 / (SEGS * GRID * GRID))

    lanes = lax.broadcasted_iota(jnp.int32, (1, 128), 1)

    def lane_of(*signed_places):
        value = jnp.zeros((1, 128), f32)
        for sign, at in signed_places:
            value = value + jnp.where(lanes == at, sign * line, 0.0)
        return jnp.sum(value, axis=1, keepdims=True)

    coeffs = [lane_of((1.0, at), (-1.0, 16 + 8 * at + 7)) for at in range(KRYLOV)]
    norm_sq = lane_of((1.0, KRYLOV), (-2.0, KRYLOV - 1), (1.0, 79))
    left = jnp.zeros((1, 128), f32)
    right = jnp.zeros((1, 128), f32)
    for at in range(KRYLOV):
        left = left + jnp.where((lanes >= 16 + 8 * at) & (lanes < 24 + 8 * at), coeffs[at], 0.0)
        right = right + jnp.where((lanes >= 16) & (lanes % 8 == at) & (lanes < 80), coeffs[at], 0.0)
        norm_sq = norm_sq - 2.0 * coeffs[at] * coeffs[at]
    norm_sq = norm_sq + jnp.sum(left * right * line, axis=1, keepdims=True)
    norm = jnp.sqrt(norm_sq)
    column = jnp.where(lanes == KRYLOV, norm, 0.0)
    for at in range(KRYLOV):
        column = jnp.where(lanes == at, coeffs[at], column)
    hess_ref[...] = column
    inverse = 1.0 / norm
    remainder = wrapped
    for at in range(KRYLOV):
        remainder = remainder - coeffs[at] * basis[at].astype(f32)
    out_ref[0] = remainder * inverse

    for source, at, rows in ((s1, 0, 256), (s2, 1, 256), (s3, 2, 256), (s5, 4, 256), (s6, 5, 256)):
        arrival(source, source, at, rows).wait_send()
    sent_a.wait_send()
    sent_b.wait_send()
    pair_done(0).wait_send()
    count_copy.wait_send()


def per_device(basis, base_grad, step_counts, shift):
    any_space = pl.BlockSpec(memory_space=pl.ANY)
    scalars = pl.BlockSpec(memory_space=pltpu.SMEM)
    f32, bf16 = jnp.float32, jnp.bfloat16
    tile = pltpu.VMEM((256, 128), f32)
    new_vector, line = pl.pallas_call(
        kernel,
        out_shape=(
            jax.ShapeDtypeStruct((1, ROWS, GRID), f32),
            jax.ShapeDtypeStruct((1, 128), f32),
        ),
        in_specs=[scalars, scalars] + [any_space] * 4,
        out_specs=(pl.BlockSpec(memory_space=pltpu.VMEM),) * 2,
        scratch_shapes=[
            pltpu.VMEM((KRYLOV, ROWS, GRID), bf16),
            pltpu.VMEM((4, ROWS, GRID), bf16),
            pltpu.VMEM(TABLE.shape, bf16),
            pltpu.VMEM((96, 128), f32),
            pltpu.VMEM((2, 1, 128), jnp.int32),
            tile, tile, tile, tile, tile,
            tile, tile, tile, tile, tile,
            pltpu.VMEM((1, SPACE, 9, 128), jnp.int32),
            pltpu.VMEM((1, SPACE, 9, 128), jnp.int32),
            pltpu.VMEM((KRYLOV, 256, 128), f32),
            pltpu.VMEM((2, 1, 128), f32),
            pltpu.VMEM((COLUMN, 1, 128), f32),
            pltpu.VMEM((PLANE, 1, 128), f32),
            pltpu.SemaphoreType.DMA((4,)),
            pltpu.SemaphoreType.DMA((10,)),
            pltpu.SemaphoreType.DMA((10,)),
            pltpu.SemaphoreType.REGULAR,
        ],
        compiler_params=pltpu.CompilerParams(
            collective_id=0, has_side_effects=True, vmem_limit_bytes=54976 * 1024
        ),
    )(
        step_counts,
        shift,
        basis[0],
        base_grad.reshape(4, ROWS, GRID),
        jnp.asarray(TABLE),
        jnp.asarray(TWIST),
    )
    return new_vector, line[0, : KRYLOV + 1]


def solution(mesh):
    in_specs = (P("seg", None, "space", None), P("seg", None, None, "space", None), P("seg"), P())
    out_specs = (P("seg", "space", None), P())
    return jax.shard_map(
        per_device, mesh=mesh, in_specs=in_specs, out_specs=out_specs, check_vma=False
    )
```

```python
import math

import jax
import jax.numpy as jnp
import ml_dtypes
import numpy as np
from jax import lax
from jax.experimental import pallas as pl
from jax.experimental.pallas import tpu as pltpu
from jax.sharding import PartitionSpec as P

MESH = pl.DeviceIdType.MESH
GRID = 1024
SPACE = 32
SEGS = 16
KRYLOV = 8
PLANE = 32
COLUMN = 16
ROWS = GRID // SPACE
HALF = math.sqrt(0.5)


def make_tables():
    tabs = {}
    small = np.arange(128)
    full = np.arange(256)
    short = np.arange(32)

    def by_owner(real, imag):
        return np.concatenate([real, imag], axis=1)

    def owner_rows(real, imag):
        return np.concatenate([real, imag], axis=0)

    def swapped(table):
        return np.concatenate([table[128:], -table[:128]], axis=0)

    angle = 2 * np.pi / 256 * ((full[:, None] * small[None, :]) % 256)
    real, imag = np.cos(angle), -np.sin(angle)
    imag[:, 0] = (-1.0) ** full
    tabs["A0"] = by_owner(real, imag)
    real, imag = 2 * np.cos(angle.T), -2 * np.sin(angle.T)
    real[0], imag[0] = 1.0, (-1.0) ** full
    tabs["B0"] = owner_rows(real, imag) / GRID
    angle = 2 * np.pi / 128 * ((small[:, None] * small[None, :]) % 128)
    cos, sin = np.cos(angle), np.sin(angle)
    tabs["A1"] = np.concatenate([by_owner(cos, -sin), by_owner(sin, cos)], 0)
    real = np.concatenate([cos, sin], 1)
    imag = np.concatenate([-sin, cos], 1)
    tabs["B1"] = owner_rows(real, imag) * 2 / GRID
    tabs["D0"] = swapped(tabs["B0"])
    tabs["D1"] = swapped(tabs["B1"])
    angle = 2 * np.pi / 32 * ((short[:, None] * short[None, :]) % 32)
    cos, sin = np.cos(angle), np.sin(angle)
    table = np.zeros((2, 5, 32, 2, 32, 4))
    for low in range(4):
        table[0, low, :, 0, :, low] = cos
        table[0, low, :, 1, :, low] = sin
        table[1, low, :, 0, :, low] = -sin
        table[1, low, :, 1, :, low] = cos
    table[0, 4, :, 1, :, 0] = cos
    table[1, 4, :, 1, :, 0] = -sin
    tabs["L1"] = table.reshape(320, 256)
    table = np.zeros((2, 32, 4, 2, 4, 32))
    for low in range(4):
        table[0, :, low, 0, low, :] = cos
        table[0, :, low, 1, low, :] = -sin
        table[1, :, low, 0, low, :] = sin
        table[1, :, low, 1, low, :] = cos
    tabs["M1"] = table.reshape(256, 256) / GRID
    for name, sign in (("L2", 1.0), ("M2", -1.0)):
        table = np.zeros((2, 4, 32, 2, 4, 32))
        for slot in range(4):
            table[0, slot, :, 0, slot, :] = cos
            table[0, slot, :, 1, slot, :] = -sign * sin
            table[1, slot, :, 0, slot, :] = sign * sin
            table[1, slot, :, 1, slot, :] = cos
        tabs[name] = table.reshape(256, 256)
    return tabs


def make_constants():
    offsets, parts, at = {}, [], 0
    for name, table in make_tables().items():
        table = table.astype(np.float32)
        high = table.astype(ml_dtypes.bfloat16)
        low = (table - high.astype(np.float32)).astype(ml_dtypes.bfloat16)
        count = table.shape[0]
        offsets[name] = (at, count)
        parts += [high, low]
        at += 2 * count
    small = np.arange(128)
    short = np.arange(32)
    twist = np.zeros((1024, 128))
    angle = 2 * np.pi / GRID * ((np.arange(1, 4)[:, None] * small[None, :]) % GRID)
    twist[0:3], twist[8:11] = np.cos(angle), np.sin(angle)
    angle = 2 * np.pi / GRID * ((short[:, None] * short[None, :]) % GRID)
    twist[16:48] = np.tile(np.cos(angle), (1, 4))
    twist[48:80] = np.tile(np.sin(angle), (1, 4))
    for slot in range(4):
        freq = 4 * small if slot == 0 else slot + 8 * small
        freq = np.where(freq < GRID // 2, freq, freq - GRID) * (8.0 / GRID)
        twist[80 + slot] = freq
    return offsets, np.concatenate(parts, 0), twist.astype(np.float32)


OFFSETS, TABLE, TWIST = make_constants()


def dot(left, right):
    return jnp.dot(left, right, preferred_element_type=jnp.float32)


def halves(value):
    high = value.astype(jnp.bfloat16)
    return high, (value - high.astype(jnp.float32)).astype(jnp.bfloat16)


def phi_triple(scaled):
    small = jnp.abs(scaled) < 0.5
    safe = jnp.where(small, jnp.ones_like(scaled), scaled)
    inverse = 1.0 / safe
    growth = jnp.exp(safe) - 1.0
    first_phi = growth * inverse
    second_phi = (first_phi - 1.0) * inverse
    series_one = jnp.zeros_like(scaled)
    series_two = jnp.zeros_like(scaled)
    for power in range(10, -1, -1):
        fact_one = float(math.factorial(power + 1))
        series_one = series_one * scaled + 1.0 / fact_one
        series_two = series_two * scaled + 1.0 / (fact_one * (power + 2))
    return (
        jnp.exp(scaled),
        jnp.where(small, series_one, first_phi),
        jnp.where(small, series_two, second_phi),
    )


def kernel(
    steps_ref, shift_ref, basis_hbm, grad_hbm, table_hbm, twist_hbm,
    out_ref, hess_ref,
    basis, grad, table, twist, counts,
    ones_out, ones_in, pair_out, pair_in, spectra,
    mine, sum_a, sum_b,
    local_sem, send_sem, recv_sem, ready,
):
    seg = lax.axis_index("seg")
    me = lax.axis_index("space")
    other = seg + 2 - 4 * (lax.rem(seg, 4) // 2)
    half, place = me // 16, lax.rem(me, 16)
    column_y, core = place // 2, lax.rem(place, 2)
    chip_x, chip_z = seg // 4, lax.rem(seg, 4) + 4 * half
    f32 = jnp.float32

    loads = [
        pltpu.make_async_copy(source, target, local_sem.at[at])
        for at, (source, target) in enumerate(
            ((basis_hbm, basis), (twist_hbm.at[pl.ds(0, 96)], twist), (table_hbm, table), (grad_hbm, grad))
        )
    ]
    for load in loads:
        load.start()

    before = lax.rem(seg + SEGS - 1, SEGS)
    before = before + 2 - 4 * (lax.rem(before, 4) // 2)
    after = lax.rem(other + 1, SEGS)

    barrier = pltpu.get_barrier_semaphore()

    def far_first(step, size):
        away = (step + 1) // 2
        return lax.rem(size + size // 2 + away * (1 - 2 * lax.rem(step, 2)), size)

    def peer_in_space(step):
        inner = lax.rem(step, 4)
        chip_y = lax.rem(column_y + far_first(step // 4, 8), 8)
        peer_core = lax.rem(core + 1 + lax.rem(inner, 2), 2)
        return 16 * (inner // 2) + 2 * chip_y + peer_core

    def peer_in_plane(step):
        peer_z = lax.rem(chip_z + far_first(step // 4, 8), 8)
        peer_x = lax.rem(chip_x + far_first(lax.rem(step, 4), 4), 4)
        return {"seg": 4 * peer_x + lax.rem(peer_z, 4), "space": 16 * (peer_z // 4) + place}

    def peer_in_column(step):
        chip_y = lax.rem(column_y + far_first(step // 2, 8), 8)
        peer_core = lax.rem(core + 1 + lax.rem(step, 2), 2)
        return {"space": 16 * half + 2 * chip_y + peer_core}

    def greet_space(step, carry):
        pl.semaphore_signal(
            barrier, inc=1, device_id={"seg": other, "space": peer_in_space(step)}, device_id_type=MESH
        )
        return carry

    def greet_plane(step, carry):
        pl.semaphore_signal(barrier, inc=1, device_id=peer_in_plane(step), device_id_type=MESH)
        return carry

    lax.fori_loop(0, SPACE, greet_space, 0)
    lax.fori_loop(0, PLANE - 1, greet_plane, 0)

    def const(name):
        at, count = OFFSETS[name]
        return table[at : at + count, :], table[at + count : at + 2 * count, :]

    def const_left(name, value):
        high, low = halves(value)
        table_high, table_low = const(name)
        both = dot(table_high, jnp.concatenate([high, low], axis=1))
        return both[:, :128] + both[:, 128:] + dot(table_low, high)

    def const_right(value, name):
        high, low = halves(value)
        table_high, table_low = const(name)
        return dot(
            jnp.concatenate([high, high, low], axis=1),
            jnp.concatenate([table_high, table_low, table_high], axis=0),
        )

    def coded(field):
        real, imag = field[:128], field[128:]
        top = jnp.max(jnp.maximum(jnp.abs(real), jnp.abs(imag)), axis=0, keepdims=True)
        level = jnp.ceil(256.0 * jnp.log2(jnp.maximum(top, 1e-30))).astype(jnp.int32) + 1
        scale = jnp.exp2(15.0 - level.astype(f32) * (1.0 / 256.0))
        high = jnp.floor(real * scale + 0.5).astype(jnp.int32)
        low = jnp.floor(imag * scale + 0.5).astype(jnp.int32)
        return (high << 16) | (low & 0xFFFF), level

    def pack(fields, source, at):
        count = len(fields)
        for which, field in enumerate(fields):
            words, level = coded(field)
            for peer in range(SPACE):
                source[at, peer, 4 * which : 4 * which + 4, :] = words[4 * peer : 4 * peer + 4]
            row = 4 * count + which
            source[at, :, row : row + 1, :] = jnp.broadcast_to(level.reshape(1, 1, 128), (SPACE, 1, 128))

    def send(source, target, at, sem, to_seg):
        def step_to(step, carry):
            peer = peer_in_space(step)
            pltpu.make_async_remote_copy(
                src_ref=source.at[at, peer],
                dst_ref=target.at[at, me],
                send_sem=send_sem.at[sem],
                recv_sem=recv_sem.at[sem],
                device_id={"seg": to_seg, "space": peer},
                device_id_type=MESH,
            ).start()
            return carry

        lax.fori_loop(0, SPACE, step_to, 0)

    def arrival(source, target, at, sem):
        return pltpu.make_async_remote_copy(
            src_ref=source.at[at],
            dst_ref=target.at[at],
            send_sem=send_sem.at[sem],
            recv_sem=recv_sem.at[sem],
            device_id={"space": me},
            device_id_type=MESH,
        )

    def received(target, at, count):
        fields = []
        for which in range(count):
            rows = [target[at, peer, 4 * which : 4 * which + 4, :] for peer in range(SPACE)]
            words = jnp.concatenate(rows, axis=0)
            row = 4 * count + which
            levels = [
                jnp.broadcast_to(target[at, peer, row : row + 1, :], (4, 128)) for peer in range(SPACE)
            ]
            scale = jnp.exp2(jnp.concatenate(levels, axis=0).astype(f32) * (1.0 / 256.0) - 15.0)
            real = (words >> 16).astype(f32) * scale
            imag = ((words << 16) >> 16).astype(f32) * scale
            fields.append(jnp.concatenate([real, imag], axis=0))
        return fields

    def send_one(field, at, to_seg):
        pack([field], ones_out, at)
        send(ones_out, ones_in, at, at, to_seg)

    def receive_one(at):
        arrival(ones_out, ones_in, at, at).wait_recv()
        return received(ones_in, at, 1)[0]

    def basis_spectra(at):
        for index in (2 * at, 2 * at + 1):
            if index == KRYLOV - 1:
                spectra[index] = weight * start_spectrum
            else:
                zero, rest = row_spectrum(basis[index].astype(f32))
                spectra[index] = weight * jnp.concatenate([zero, rest], axis=0).T

    def row_spectrum(field):
        group = [field[:, 128 * at : 128 * at + 128] for at in range(8)]
        plus = [group[at] + group[at + 4] for at in range(4)]
        minus = [group[at] - group[at + 4] for at in range(4)]
        zero = jnp.concatenate([plus[0] + plus[2], plus[1] + plus[3]], axis=1)
        inner = HALF * (minus[1] - minus[3])
        outer = HALF * (minus[1] + minus[3])
        pairs = (
            (minus[0] + inner, -(minus[2] + outer)),
            (plus[0] - plus[2], plus[3] - plus[1]),
            (minus[0] - inner, minus[2] - outer),
        )
        rest = []
        for at, (real, imag) in enumerate(pairs):
            cos, sin = twist[at : at + 1, :], twist[8 + at : 9 + at, :]
            rest.append(
                jnp.concatenate([real * cos + imag * sin, imag * cos - real * sin], axis=1)
            )
        return const_right(zero, "A0"), const_right(jnp.concatenate(rest, axis=0), "A1")

    def row_field(zero, rest):
        turned = []
        for at in range(3):
            real, imag = rest[32 * at : 32 * at + 32, :128], rest[32 * at : 32 * at + 32, 128:]
            cos, sin = twist[at : at + 1, :], twist[8 + at : 9 + at, :]
            turned.append((real * cos - imag * sin, real * sin + imag * cos))
        (re1, im1), (re2, im2), (re3, im3) = turned
        even, odd = zero[:, :128], zero[:, 128:]
        sums = (even + re2, odd - im2, even - re2, odd + im2)
        differences = (
            re1 + re3,
            HALF * ((re1 - im1) - (re3 + im3)),
            im3 - im1,
            HALF * ((re3 - im3) - (re1 + im1)),
        )
        pieces = [sums[at] + differences[at] for at in range(4)]
        pieces += [sums[at] - differences[at] for at in range(4)]
        return jnp.concatenate(pieces, axis=1)

    def rows_forward(field):
        zero, rest = row_spectrum(field)
        return jnp.concatenate([zero, rest], axis=0).T

    def rows_inverse(spectrum):
        turned = spectrum.T
        return row_field(const_right(turned[:32], "B0"), const_right(turned[32:], "B1"))

    def stacked(value):
        return jnp.concatenate([value] * 5, axis=0)

    lane = lax.broadcasted_iota(jnp.int32, (160, 128), 1)
    row = lax.broadcasted_iota(jnp.int32, (160, 128), 0)
    anchor = jnp.where((lane[:32] < 32) & (me == 0), 1.0, 0.0).astype(f32)

    def columns_forward(received):
        value = const_left("L1", received)
        real, imag = value[:160], value[160:]
        real = jnp.concatenate([real[:32] + anchor * imag[128:], real[32:]], axis=0)
        imag = jnp.concatenate([imag[:32] - anchor * value[128:160], imag[32:]], axis=0)
        cos, sin = stacked(twist[16:48, :]), stacked(twist[48:80, :])
        turned = jnp.concatenate([real * cos + imag * sin, imag * cos - real * sin], axis=1)
        value = const_right(turned, "L2")
        return value[:, :128], value[:, 128:]

    def columns_inverse(real, imag):
        value = const_right(jnp.concatenate([real, imag], axis=1), "M2")
        real, imag = value[:, :128], value[:, 128:]
        cos, sin = stacked(twist[16:48, :]), stacked(twist[48:80, :])
        real, imag = real * cos - imag * sin, real * sin + imag * cos
        value = jnp.concatenate(
            [real[:32] - anchor * imag[128:], real[32:128], imag[:32] + anchor * real[128:], imag[32:128]],
            axis=0,
        )
        return const_left("M1", value)

    pair_row = lax.broadcasted_iota(jnp.int32, (256, 128), 0)
    pair_lane = lax.broadcasted_iota(jnp.int32, (256, 128), 1)
    alone = (pair_row % 128 == 0) & (pair_lane < 32)
    weight = jnp.where(alone, 1.0 / GRID, 2.0 / GRID).astype(f32)

    loads[0].wait()
    loads[1].wait()
    loads[2].wait()
    start = basis[KRYLOV - 1].astype(f32)
    zero, rest = row_spectrum(start)
    start_spectrum = jnp.concatenate([zero, rest], axis=0).T
    pack([start_spectrum], ones_out, 0)
    pl.semaphore_wait(barrier, SPACE + PLANE - 1)
    send(ones_out, ones_in, 0, 0, other)
    counts[0] = jnp.full((1, 128), steps_ref[0], jnp.int32)
    count_copy = pltpu.make_async_remote_copy(
        src_ref=counts.at[0],
        dst_ref=counts.at[1],
        send_sem=send_sem.at[8],
        recv_sem=recv_sem.at[8],
        device_id={"seg": other},
        device_id_type=MESH,
    )
    count_copy.start()
    basis_spectra(0)

    waves = [
        jnp.concatenate([twist[80 + at : 81 + at, :]] * 2, axis=1)
        for at in range(4)
    ]
    lifted = jnp.concatenate([rest[32 * at : 32 * at + 32] * waves[at + 1] for at in range(3)], axis=0)
    grad_y = row_field(const_right(zero * waves[0], "D0"), const_right(lifted, "D1"))

    slot = lane // 32
    low = row // 32
    freq_x = row % 32 + 32 * (lane % 32)
    base = 4 * me + low
    freq_y = jnp.where(low == 4, GRID // 2, jnp.where(slot == 0, 4 * base, slot + 8 * base))
    signed_x = jnp.where(freq_x < GRID // 2, freq_x, freq_x - GRID)
    signed_y = jnp.where(freq_y < GRID // 2, freq_y, freq_y - GRID)
    wave_x = signed_x.astype(f32) * (8.0 / GRID)
    wave_y = signed_y.astype(f32) * (8.0 / GRID)
    deriv_x = jnp.where(signed_x == -(GRID // 2), 0.0, wave_x)
    deriv_y = jnp.where(signed_y == -(GRID // 2), 0.0, wave_y)
    squared = wave_x * wave_x + wave_y * wave_y
    count_copy.wait_recv()
    step_size = 0.01 * counts[1].astype(f32)
    decay, phi_one, phi_two = phi_triple((squared - squared * squared) * step_size)
    phi_one = step_size * phi_one
    phi_two = step_size * phi_two

    state_re, state_im = columns_forward(receive_one(0))

    send_one(columns_inverse(-deriv_x * state_im, deriv_x * state_re), 1, other)
    basis_spectra(1)
    loads[3].wait()
    part_y = grad[1].astype(f32) * grad_y
    part_x = -grad[0].astype(f32)
    slope = receive_one(1)
    pl.semaphore_signal(ready, inc=1, device_id={"seg": before}, device_id_type=MESH)
    term = part_x * rows_inverse(slope) - part_y

    send_one(rows_forward(term), 2, other)
    basis_spectra(2)
    flat = basis[...].reshape(KRYLOV * ROWS, GRID)
    gram = lax.dot_general(flat, flat, (((1,), (1,)), ((), ())), preferred_element_type=f32)
    gram_row = lax.broadcasted_iota(jnp.int32, (256, 256), 0)
    gram_lane = lax.broadcasted_iota(jnp.int32, (256, 256), 1)
    gram = jnp.where(gram_row % 32 == gram_lane % 32, gram, 0.0)
    gram = jnp.concatenate(
        [jnp.sum(gram[32 * at : 32 * at + 32], axis=0, keepdims=True) for at in range(8)], axis=0
    )
    spot_row = lax.broadcasted_iota(jnp.int32, (8, 128), 0)
    spot_lane = lax.broadcasted_iota(jnp.int32, (8, 128), 1)
    gram_sums = jnp.zeros((8, 128), f32)
    for at in range(8):
        part = jnp.sum(jnp.where(gram_lane[:8] // 32 == at, gram, 0.0), axis=1, keepdims=True)
        gram_sums = gram_sums + jnp.where(spot_lane == 16 + 8 * spot_row + at, part, 0.0)
    gram_sums = jnp.sum(gram_sums, axis=0, keepdims=True)
    term_re, term_im = columns_forward(receive_one(2))
    middle_re = decay * state_re + phi_one * term_re
    middle_im = decay * state_im + phi_one * term_im

    toward_x = columns_inverse(-deriv_x * middle_im, deriv_x * middle_re)
    toward_y = columns_inverse(-deriv_y * middle_im, deriv_y * middle_re)
    pack([toward_x, toward_y], pair_out, 0)
    send(pair_out, pair_in, 0, 5, other)
    basis_spectra(3)
    offset = (freq_x * shift_ref[0] + freq_y * shift_ref[1]) & (GRID - 1)
    angle = (2.0 * math.pi / GRID) * offset.astype(f32)
    is_last = other == SEGS - 1
    cosine = jnp.where(is_last, jnp.cos(angle), 1.0)
    sine = jnp.where(is_last, jnp.sin(angle), 0.0)
    arrival(pair_out, pair_in, 0, 5).wait_recv()
    got_x, got_y = received(pair_in, 0, 2)
    term = -(grad[2].astype(f32) * rows_inverse(got_x) + grad[3].astype(f32) * rows_inverse(got_y))

    send_one(rows_forward(term), 3, other)
    kept_re = middle_re - phi_two * term_re
    kept_im = middle_im - phi_two * term_im
    term_re, term_im = columns_forward(receive_one(3))
    state_re = kept_re + phi_two * term_re
    state_im = kept_im + phi_two * term_im

    flow = columns_inverse(cosine * state_re + sine * state_im, cosine * state_im - sine * state_re)
    pl.semaphore_wait(ready, 1)
    send_one(flow, 4, after)
    flow = receive_one(4)

    def folded(value):
        total = value[:8]
        for at in range(1, 32):
            total = total + value[8 * at : 8 * at + 8]
        return jnp.sum(total, axis=0, keepdims=True)

    lines = [folded(flow * spectra[at]) for at in range(KRYLOV)]
    lines.append(folded(flow * flow * weight))
    lines.append(jnp.zeros((7, 128), f32))
    sums = jnp.sum(jnp.concatenate(lines, axis=0), axis=1, keepdims=True)
    spot_row = lax.broadcasted_iota(jnp.int32, (16, 128), 0)
    spot_lane = lax.broadcasted_iota(jnp.int32, (16, 128), 1)
    line = jnp.sum(jnp.where(spot_row == spot_lane, sums, 0.0), axis=0, keepdims=True) + gram_sums

    def spread(target, peer_of, own, count, at):
        target[own] = mine[at]

        def step_to(step, carry):
            pltpu.make_async_remote_copy(
                src_ref=mine.at[at],
                dst_ref=target.at[own],
                send_sem=send_sem.at[6 + at],
                recv_sem=recv_sem.at[6 + at],
                device_id=peer_of(step),
                device_id_type=MESH,
            ).start()
            return carry

        lax.fori_loop(0, count - 1, step_to, 0)
        return pltpu.make_async_remote_copy(
            src_ref=target.at[pl.ds(0, count - 1)],
            dst_ref=target.at[pl.ds(0, count - 1)],
            send_sem=send_sem.at[6 + at],
            recv_sem=recv_sem.at[6 + at],
            device_id={"seg": other},
            device_id_type=MESH,
        )

    mine[0] = line
    sent_a = spread(sum_a, peer_in_column, place, COLUMN, 0)
    wrapped = rows_inverse(flow) - start
    sent_a.wait_recv()
    mine[1] = jnp.sum(sum_a[...], axis=0)
    sent_b = spread(sum_b, peer_in_plane, 8 * chip_x + chip_z, PLANE, 1)
    sent_b.wait_recv()
    line = jnp.sum(sum_b[...], axis=0) * (1.0 / (SEGS * GRID * GRID))

    lanes = lax.broadcasted_iota(jnp.int32, (1, 128), 1)

    def lane_of(*signed_places):
        value = jnp.zeros((1, 128), f32)
        for sign, at in signed_places:
            value = value + jnp.where(lanes == at, sign * line, 0.0)
        return jnp.sum(value, axis=1, keepdims=True)

    coeffs = [lane_of((1.0, at), (-1.0, 16 + 8 * at + 7)) for at in range(KRYLOV)]
    norm_sq = lane_of((1.0, KRYLOV), (-2.0, KRYLOV - 1), (1.0, 79))
    left = jnp.zeros((1, 128), f32)
    right = jnp.zeros((1, 128), f32)
    for at in range(KRYLOV):
        left = left + jnp.where((lanes >= 16 + 8 * at) & (lanes < 24 + 8 * at), coeffs[at], 0.0)
        right = right + jnp.where((lanes >= 16) & (lanes % 8 == at) & (lanes < 80), coeffs[at], 0.0)
        norm_sq = norm_sq - 2.0 * coeffs[at] * coeffs[at]
    norm_sq = norm_sq + jnp.sum(left * right * line, axis=1, keepdims=True)
    norm = jnp.sqrt(norm_sq)
    column = jnp.where(lanes == KRYLOV, norm, 0.0)
    for at in range(KRYLOV):
        column = jnp.where(lanes == at, coeffs[at], column)
    hess_ref[...] = column
    inverse = 1.0 / norm
    remainder = wrapped
    for at in range(KRYLOV):
        remainder = remainder - coeffs[at] * basis[at].astype(f32)
    out_ref[0] = remainder * inverse

    for at in range(5):
        arrival(ones_out, ones_in, at, at).wait_send()
    arrival(pair_out, pair_in, 0, 5).wait_send()
    sent_a.wait_send()
    sent_b.wait_send()
    count_copy.wait_send()


def per_device(basis, base_grad, step_counts, shift):
    any_space = pl.BlockSpec(memory_space=pl.ANY)
    scalars = pl.BlockSpec(memory_space=pltpu.SMEM)
    f32, bf16 = jnp.float32, jnp.bfloat16
    new_vector, line = pl.pallas_call(
        kernel,
        out_shape=(
            jax.ShapeDtypeStruct((1, ROWS, GRID), f32),
            jax.ShapeDtypeStruct((1, 128), f32),
        ),
        in_specs=[scalars, scalars] + [any_space] * 4,
        out_specs=(pl.BlockSpec(memory_space=pltpu.VMEM),) * 2,
        scratch_shapes=[
            pltpu.VMEM((KRYLOV, ROWS, GRID), bf16),
            pltpu.VMEM((4, ROWS, GRID), bf16),
            pltpu.VMEM(TABLE.shape, bf16),
            pltpu.VMEM((96, 128), f32),
            pltpu.VMEM((2, 1, 128), jnp.int32),
            pltpu.VMEM((5, SPACE, 5, 128), jnp.int32),
            pltpu.VMEM((5, SPACE, 5, 128), jnp.int32),
            pltpu.VMEM((1, SPACE, 10, 128), jnp.int32),
            pltpu.VMEM((1, SPACE, 10, 128), jnp.int32),
            pltpu.VMEM((KRYLOV, 256, 128), f32),
            pltpu.VMEM((2, 1, 128), f32),
            pltpu.VMEM((COLUMN, 1, 128), f32),
            pltpu.VMEM((PLANE, 1, 128), f32),
            pltpu.SemaphoreType.DMA((4,)),
            pltpu.SemaphoreType.DMA((9,)),
            pltpu.SemaphoreType.DMA((9,)),
            pltpu.SemaphoreType.REGULAR,
        ],
        compiler_params=pltpu.CompilerParams(
            collective_id=0, has_side_effects=True, vmem_limit_bytes=54976 * 1024
        ),
    )(
        step_counts,
        shift,
        basis[0],
        base_grad.reshape(4, ROWS, GRID),
        jnp.asarray(TABLE),
        jnp.asarray(TWIST),
    )
    return new_vector, line[0, : KRYLOV + 1]


def solution(mesh):
    in_specs = (P("seg", None, "space", None), P("seg", None, None, "space", None), P("seg"), P())
    out_specs = (P("seg", "space", None), P())
    return jax.shard_map(
        per_device, mesh=mesh, in_specs=in_specs, out_specs=out_specs, check_vma=False
    )
```

```python
import math

import jax
import jax.numpy as jnp
import ml_dtypes
import numpy as np
from jax import lax
from jax.experimental import pallas as pl
from jax.experimental.pallas import tpu as pltpu
from jax.sharding import PartitionSpec as P

MESH = pl.DeviceIdType.MESH
GRID = 1024
SPACE = 32
SEGS = 16
KRYLOV = 8
PLANE = 32
COLUMN = 16
ROWS = GRID // SPACE
HALF = math.sqrt(0.5)


def make_tables():
    tabs = {}
    small = np.arange(128)
    full = np.arange(256)
    short = np.arange(32)

    def by_owner(real, imag):
        return np.concatenate([real, imag], axis=1)

    def owner_rows(real, imag):
        return np.concatenate([real, imag], axis=0)

    def swapped(table):
        return np.concatenate([table[128:], -table[:128]], axis=0)

    angle = 2 * np.pi / 256 * ((full[:, None] * small[None, :]) % 256)
    real, imag = np.cos(angle), -np.sin(angle)
    imag[:, 0] = (-1.0) ** full
    tabs["A0"] = by_owner(real, imag)
    real, imag = 2 * np.cos(angle.T), -2 * np.sin(angle.T)
    real[0], imag[0] = 1.0, (-1.0) ** full
    tabs["B0"] = owner_rows(real, imag) / GRID
    angle = 2 * np.pi / 128 * ((small[:, None] * small[None, :]) % 128)
    cos, sin = np.cos(angle), np.sin(angle)
    tabs["A1"] = np.concatenate([by_owner(cos, -sin), by_owner(sin, cos)], 0)
    real = np.concatenate([cos, sin], 1)
    imag = np.concatenate([-sin, cos], 1)
    tabs["B1"] = owner_rows(real, imag) * 2 / GRID
    tabs["D0"] = swapped(tabs["B0"])
    tabs["D1"] = swapped(tabs["B1"])
    angle = 2 * np.pi / 32 * ((short[:, None] * short[None, :]) % 32)
    cos, sin = np.cos(angle), np.sin(angle)
    table = np.zeros((2, 5, 32, 2, 32, 4))
    for low in range(4):
        table[0, low, :, 0, :, low] = cos
        table[0, low, :, 1, :, low] = sin
        table[1, low, :, 0, :, low] = -sin
        table[1, low, :, 1, :, low] = cos
    table[0, 4, :, 1, :, 0] = cos
    table[1, 4, :, 1, :, 0] = -sin
    tabs["L1"] = table.reshape(320, 256)
    table = np.zeros((2, 32, 4, 2, 4, 32))
    for low in range(4):
        table[0, :, low, 0, low, :] = cos
        table[0, :, low, 1, low, :] = -sin
        table[1, :, low, 0, low, :] = sin
        table[1, :, low, 1, low, :] = cos
    tabs["M1"] = table.reshape(256, 256) / GRID
    for name, sign in (("L2", 1.0), ("M2", -1.0)):
        table = np.zeros((2, 4, 32, 2, 4, 32))
        for slot in range(4):
            table[0, slot, :, 0, slot, :] = cos
            table[0, slot, :, 1, slot, :] = -sign * sin
            table[1, slot, :, 0, slot, :] = sign * sin
            table[1, slot, :, 1, slot, :] = cos
        tabs[name] = table.reshape(256, 256)
    return tabs


def make_constants():
    offsets, parts, at = {}, [], 0
    for name, table in make_tables().items():
        table = table.astype(np.float32)
        high = table.astype(ml_dtypes.bfloat16)
        low = (table - high.astype(np.float32)).astype(ml_dtypes.bfloat16)
        count = table.shape[0]
        offsets[name] = (at, count)
        parts += [high, low]
        at += 2 * count
    small = np.arange(128)
    short = np.arange(32)
    twist = np.zeros((1024, 128))
    angle = 2 * np.pi / GRID * ((np.arange(1, 4)[:, None] * small[None, :]) % GRID)
    twist[0:3], twist[8:11] = np.cos(angle), np.sin(angle)
    angle = 2 * np.pi / GRID * ((short[:, None] * short[None, :]) % GRID)
    twist[16:48] = np.tile(np.cos(angle), (1, 4))
    twist[48:80] = np.tile(np.sin(angle), (1, 4))
    for slot in range(4):
        freq = 4 * small if slot == 0 else slot + 8 * small
        freq = np.where(freq < GRID // 2, freq, freq - GRID) * (8.0 / GRID)
        twist[80 + slot] = freq
    return offsets, np.concatenate(parts, 0), twist.astype(np.float32)


OFFSETS, TABLE, TWIST = make_constants()


def dot(left, right):
    return jnp.dot(left, right, preferred_element_type=jnp.float32)


def halves(value):
    high = value.astype(jnp.bfloat16)
    return high, (value - high.astype(jnp.float32)).astype(jnp.bfloat16)


def phi_triple(scaled):
    small = jnp.abs(scaled) < 0.5
    safe = jnp.where(small, jnp.ones_like(scaled), scaled)
    inverse = 1.0 / safe
    growth = jnp.exp(safe) - 1.0
    first_phi = growth * inverse
    second_phi = (first_phi - 1.0) * inverse
    series_one = jnp.zeros_like(scaled)
    series_two = jnp.zeros_like(scaled)
    for power in range(10, -1, -1):
        fact_one = float(math.factorial(power + 1))
        series_one = series_one * scaled + 1.0 / fact_one
        series_two = series_two * scaled + 1.0 / (fact_one * (power + 2))
    return (
        jnp.exp(scaled),
        jnp.where(small, series_one, first_phi),
        jnp.where(small, series_two, second_phi),
    )


def kernel(
    steps_ref, shift_ref, basis_hbm, grad_hbm, table_hbm, twist_hbm,
    out_ref, hess_ref,
    basis, grad, table, twist, counts,
    ones_out, ones_in, pair_out, pair_in, spectra,
    mine, sum_a, sum_b,
    local_sem, send_sem, recv_sem, ready, plane,
):
    seg = lax.axis_index("seg")
    me = lax.axis_index("space")
    other = seg + 2 - 4 * (lax.rem(seg, 4) // 2)
    half, place = me // 16, lax.rem(me, 16)
    column_y, core = place // 2, lax.rem(place, 2)
    chip_x, chip_z = seg // 4, lax.rem(seg, 4) + 4 * half
    f32 = jnp.float32

    loads = [
        pltpu.make_async_copy(source, target, local_sem.at[at])
        for at, (source, target) in enumerate(
            ((basis_hbm, basis), (twist_hbm.at[pl.ds(0, 96)], twist), (table_hbm, table), (grad_hbm, grad))
        )
    ]
    before = lax.rem(seg + SEGS - 1, SEGS)
    before = before + 2 - 4 * (lax.rem(before, 4) // 2)
    after = lax.rem(other + 1, SEGS)

    barrier = pltpu.get_barrier_semaphore()

    def far_first(step, size):
        away = (step + 1) // 2
        return lax.rem(size + size // 2 + away * (1 - 2 * lax.rem(step, 2)), size)

    def peers_in_space(step):
        chip_y = 2 * lax.rem(column_y + far_first(step, 8), 8)
        return [16 * upper + chip_y + peer_core for upper in (0, 1) for peer_core in (1 - core, core)]

    def peers_in_plane(step):
        peer_z = lax.rem(chip_z + far_first(step, 8), 8)
        inner, upper = lax.rem(peer_z, 4), 16 * (peer_z // 4) + place
        return [
            {"seg": 4 * lax.rem(chip_x + away, 4) + inner, "space": upper} for away in (2, 1, 3, 0)
        ]

    def peers_in_column(step):
        chip_y = 16 * half + 2 * lax.rem(column_y + far_first(step, 8), 8)
        return [{"space": chip_y + peer_core} for peer_core in (1 - core, core)]

    def greet_space(step, carry):
        for peer in peers_in_space(step):
            pl.semaphore_signal(
                barrier, inc=1, device_id={"seg": other, "space": peer}, device_id_type=MESH
            )
        return carry

    def line_x(step):
        return {"seg": 4 * lax.rem(chip_x + far_first(step, 4), 4) + lax.rem(seg, 4)}

    def greet_x(step, carry):
        pl.semaphore_signal(barrier, inc=1, device_id=line_x(step), device_id_type=MESH)
        return carry

    def greet_z(step, carry):
        peer_z = lax.rem(chip_z + far_first(step, 8), 8)
        peer = {"seg": 4 * chip_x + lax.rem(peer_z, 4), "space": 16 * (peer_z // 4) + place}
        pl.semaphore_signal(barrier, inc=1, device_id=peer, device_id_type=MESH)
        return carry

    def tell_x(step, carry):
        pl.semaphore_signal(plane, inc=1, device_id=line_x(step), device_id_type=MESH)
        return carry

    lax.fori_loop(0, SPACE // 4, greet_space, 0)
    lax.fori_loop(0, 7, greet_z, 0)
    lax.fori_loop(0, 3, greet_x, 0)
    for load in loads:
        load.start()

    def const(name):
        at, count = OFFSETS[name]
        return table[at : at + count, :], table[at + count : at + 2 * count, :]

    def const_left(name, value):
        high, low = halves(value)
        table_high, table_low = const(name)
        both = dot(table_high, jnp.concatenate([high, low], axis=1))
        return both[:, :128] + both[:, 128:] + dot(table_low, high)

    def const_right(value, name):
        high, low = halves(value)
        table_high, table_low = const(name)
        return dot(
            jnp.concatenate([high, high, low], axis=1),
            jnp.concatenate([table_high, table_low, table_high], axis=0),
        )

    def coded(field):
        real, imag = field[:128], field[128:]
        top = jnp.max(jnp.maximum(jnp.abs(real), jnp.abs(imag)), axis=0, keepdims=True)
        level = jnp.ceil(256.0 * jnp.log2(jnp.maximum(top, 1e-30))).astype(jnp.int32) + 1
        scale = jnp.exp2(15.0 - level.astype(f32) * (1.0 / 256.0))
        high = jnp.floor(real * scale + 0.5).astype(jnp.int32)
        low = jnp.floor(imag * scale + 0.5).astype(jnp.int32)
        return (high << 16) | (low & 0xFFFF), level

    def pack(fields, source, at):
        count = len(fields)
        for which, field in enumerate(fields):
            words, level = coded(field)
            for peer in range(SPACE):
                source[at, peer, 4 * which : 4 * which + 4, :] = words[4 * peer : 4 * peer + 4]
            row = 4 * count + which
            source[at, :, row : row + 1, :] = jnp.broadcast_to(level.reshape(1, 1, 128), (SPACE, 1, 128))

    def send(source, target, at, sem, to_seg):
        def step_to(step, carry):
            for peer in peers_in_space(step):
                pltpu.make_async_remote_copy(
                    src_ref=source.at[at, peer],
                    dst_ref=target.at[at, me],
                    send_sem=send_sem.at[sem],
                    recv_sem=recv_sem.at[sem],
                    device_id={"seg": to_seg, "space": peer},
                    device_id_type=MESH,
                ).start()
            return carry

        lax.fori_loop(0, SPACE // 4, step_to, 0)

    def arrival(source, target, at, sem):
        return pltpu.make_async_remote_copy(
            src_ref=source.at[at],
            dst_ref=target.at[at],
            send_sem=send_sem.at[sem],
            recv_sem=recv_sem.at[sem],
            device_id={"space": me},
            device_id_type=MESH,
        )

    def received(target, at, count):
        fields = []
        for which in range(count):
            rows = [target[at, peer, 4 * which : 4 * which + 4, :] for peer in range(SPACE)]
            words = jnp.concatenate(rows, axis=0)
            row = 4 * count + which
            levels = [
                jnp.broadcast_to(target[at, peer, row : row + 1, :], (4, 128)) for peer in range(SPACE)
            ]
            scale = jnp.exp2(jnp.concatenate(levels, axis=0).astype(f32) * (1.0 / 256.0) - 15.0)
            real = (words >> 16).astype(f32) * scale
            imag = ((words << 16) >> 16).astype(f32) * scale
            fields.append(jnp.concatenate([real, imag], axis=0))
        return fields

    def send_one(field, at, to_seg):
        pack([field], ones_out, at)
        send(ones_out, ones_in, at, at, to_seg)

    def receive_one(at):
        arrival(ones_out, ones_in, at, at).wait_recv()
        return received(ones_in, at, 1)[0]

    def basis_spectra(at):
        for index in (2 * at, 2 * at + 1):
            if index == KRYLOV - 1:
                spectra[index] = weight * start_spectrum
            else:
                zero, rest = row_spectrum(basis[index].astype(f32))
                spectra[index] = weight * jnp.concatenate([zero, rest], axis=0).T

    def row_spectrum(field):
        group = [field[:, 128 * at : 128 * at + 128] for at in range(8)]
        plus = [group[at] + group[at + 4] for at in range(4)]
        minus = [group[at] - group[at + 4] for at in range(4)]
        zero = jnp.concatenate([plus[0] + plus[2], plus[1] + plus[3]], axis=1)
        inner = HALF * (minus[1] - minus[3])
        outer = HALF * (minus[1] + minus[3])
        pairs = (
            (minus[0] + inner, -(minus[2] + outer)),
            (plus[0] - plus[2], plus[3] - plus[1]),
            (minus[0] - inner, minus[2] - outer),
        )
        rest = []
        for at, (real, imag) in enumerate(pairs):
            cos, sin = twist[at : at + 1, :], twist[8 + at : 9 + at, :]
            rest.append(
                jnp.concatenate([real * cos + imag * sin, imag * cos - real * sin], axis=1)
            )
        return const_right(zero, "A0"), const_right(jnp.concatenate(rest, axis=0), "A1")

    def row_field(zero, rest):
        turned = []
        for at in range(3):
            real, imag = rest[32 * at : 32 * at + 32, :128], rest[32 * at : 32 * at + 32, 128:]
            cos, sin = twist[at : at + 1, :], twist[8 + at : 9 + at, :]
            turned.append((real * cos - imag * sin, real * sin + imag * cos))
        (re1, im1), (re2, im2), (re3, im3) = turned
        even, odd = zero[:, :128], zero[:, 128:]
        sums = (even + re2, odd - im2, even - re2, odd + im2)
        differences = (
            re1 + re3,
            HALF * ((re1 - im1) - (re3 + im3)),
            im3 - im1,
            HALF * ((re3 - im3) - (re1 + im1)),
        )
        pieces = [sums[at] + differences[at] for at in range(4)]
        pieces += [sums[at] - differences[at] for at in range(4)]
        return jnp.concatenate(pieces, axis=1)

    def rows_forward(field):
        zero, rest = row_spectrum(field)
        return jnp.concatenate([zero, rest], axis=0).T

    def rows_inverse(spectrum):
        turned = spectrum.T
        return row_field(const_right(turned[:32], "B0"), const_right(turned[32:], "B1"))

    def stacked(value):
        return jnp.concatenate([value] * 5, axis=0)

    lane = lax.broadcasted_iota(jnp.int32, (160, 128), 1)
    row = lax.broadcasted_iota(jnp.int32, (160, 128), 0)
    anchor = jnp.where((lane[:32] < 32) & (me == 0), 1.0, 0.0).astype(f32)

    def columns_forward(received):
        value = const_left("L1", received)
        real, imag = value[:160], value[160:]
        real = jnp.concatenate([real[:32] + anchor * imag[128:], real[32:]], axis=0)
        imag = jnp.concatenate([imag[:32] - anchor * value[128:160], imag[32:]], axis=0)
        cos, sin = stacked(twist[16:48, :]), stacked(twist[48:80, :])
        turned = jnp.concatenate([real * cos + imag * sin, imag * cos - real * sin], axis=1)
        value = const_right(turned, "L2")
        return value[:, :128], value[:, 128:]

    def columns_inverse(real, imag):
        value = const_right(jnp.concatenate([real, imag], axis=1), "M2")
        real, imag = value[:, :128], value[:, 128:]
        cos, sin = stacked(twist[16:48, :]), stacked(twist[48:80, :])
        real, imag = real * cos - imag * sin, real * sin + imag * cos
        value = jnp.concatenate(
            [real[:32] - anchor * imag[128:], real[32:128], imag[:32] + anchor * real[128:], imag[32:128]],
            axis=0,
        )
        return const_left("M1", value)

    pair_row = lax.broadcasted_iota(jnp.int32, (256, 128), 0)
    pair_lane = lax.broadcasted_iota(jnp.int32, (256, 128), 1)
    alone = (pair_row % 128 == 0) & (pair_lane < 32)
    weight = jnp.where(alone, 1.0 / GRID, 2.0 / GRID).astype(f32)

    loads[0].wait()
    loads[1].wait()
    loads[2].wait()
    start = basis[KRYLOV - 1].astype(f32)
    zero, rest = row_spectrum(start)
    start_spectrum = jnp.concatenate([zero, rest], axis=0).T
    pack([start_spectrum], ones_out, 0)
    pl.semaphore_wait(barrier, SPACE + 10)
    send(ones_out, ones_in, 0, 0, other)
    lax.fori_loop(0, 3, tell_x, 0)
    counts[0] = jnp.full((1, 128), steps_ref[0], jnp.int32)
    count_copy = pltpu.make_async_remote_copy(
        src_ref=counts.at[0],
        dst_ref=counts.at[1],
        send_sem=send_sem.at[8],
        recv_sem=recv_sem.at[8],
        device_id={"seg": other},
        device_id_type=MESH,
    )
    count_copy.start()
    basis_spectra(0)

    waves = [
        jnp.concatenate([twist[80 + at : 81 + at, :]] * 2, axis=1)
        for at in range(4)
    ]
    lifted = jnp.concatenate([rest[32 * at : 32 * at + 32] * waves[at + 1] for at in range(3)], axis=0)
    grad_y = row_field(const_right(zero * waves[0], "D0"), const_right(lifted, "D1"))

    slot = lane // 32
    low = row // 32
    freq_x = row % 32 + 32 * (lane % 32)
    base = 4 * me + low
    freq_y = jnp.where(low == 4, GRID // 2, jnp.where(slot == 0, 4 * base, slot + 8 * base))
    signed_x = jnp.where(freq_x < GRID // 2, freq_x, freq_x - GRID)
    signed_y = jnp.where(freq_y < GRID // 2, freq_y, freq_y - GRID)
    wave_x = signed_x.astype(f32) * (8.0 / GRID)
    wave_y = signed_y.astype(f32) * (8.0 / GRID)
    deriv_x = jnp.where(signed_x == -(GRID // 2), 0.0, wave_x)
    deriv_y = jnp.where(signed_y == -(GRID // 2), 0.0, wave_y)
    squared = wave_x * wave_x + wave_y * wave_y
    count_copy.wait_recv()
    step_size = 0.01 * counts[1].astype(f32)
    decay, phi_one, phi_two = phi_triple((squared - squared * squared) * step_size)
    phi_one = step_size * phi_one
    phi_two = step_size * phi_two

    state_re, state_im = columns_forward(receive_one(0))

    send_one(columns_inverse(-deriv_x * state_im, deriv_x * state_re), 1, other)
    basis_spectra(1)
    loads[3].wait()
    part_y = grad[1].astype(f32) * grad_y
    part_x = -grad[0].astype(f32)
    slope = receive_one(1)
    pl.semaphore_wait(plane, 3)
    pl.semaphore_signal(ready, inc=1, device_id={"seg": before}, device_id_type=MESH)
    term = part_x * rows_inverse(slope) - part_y

    send_one(rows_forward(term), 2, other)
    basis_spectra(2)
    flat = basis[...].reshape(KRYLOV * ROWS, GRID)
    gram = lax.dot_general(flat, flat, (((1,), (1,)), ((), ())), preferred_element_type=f32)
    gram_row = lax.broadcasted_iota(jnp.int32, (256, 256), 0)
    gram_lane = lax.broadcasted_iota(jnp.int32, (256, 256), 1)
    gram = jnp.where(gram_row % 32 == gram_lane % 32, gram, 0.0)
    gram = jnp.concatenate(
        [jnp.sum(gram[32 * at : 32 * at + 32], axis=0, keepdims=True) for at in range(8)], axis=0
    )
    spot_row = lax.broadcasted_iota(jnp.int32, (8, 128), 0)
    spot_lane = lax.broadcasted_iota(jnp.int32, (8, 128), 1)
    gram_sums = jnp.zeros((8, 128), f32)
    for at in range(8):
        part = jnp.sum(jnp.where(gram_lane[:8] // 32 == at, gram, 0.0), axis=1, keepdims=True)
        gram_sums = gram_sums + jnp.where(spot_lane == 16 + 8 * spot_row + at, part, 0.0)
    gram_sums = jnp.sum(gram_sums, axis=0, keepdims=True)
    term_re, term_im = columns_forward(receive_one(2))
    middle_re = decay * state_re + phi_one * term_re
    middle_im = decay * state_im + phi_one * term_im

    toward_x = columns_inverse(-deriv_x * middle_im, deriv_x * middle_re)
    toward_y = columns_inverse(-deriv_y * middle_im, deriv_y * middle_re)
    pack([toward_x, toward_y], pair_out, 0)
    send(pair_out, pair_in, 0, 5, other)
    basis_spectra(3)
    offset = (freq_x * shift_ref[0] + freq_y * shift_ref[1]) & (GRID - 1)
    angle = (2.0 * math.pi / GRID) * offset.astype(f32)
    is_last = other == SEGS - 1
    cosine = jnp.where(is_last, jnp.cos(angle), 1.0)
    sine = jnp.where(is_last, jnp.sin(angle), 0.0)
    arrival(pair_out, pair_in, 0, 5).wait_recv()
    got_x, got_y = received(pair_in, 0, 2)
    term = -(grad[2].astype(f32) * rows_inverse(got_x) + grad[3].astype(f32) * rows_inverse(got_y))

    send_one(rows_forward(term), 3, other)
    kept_re = middle_re - phi_two * term_re
    kept_im = middle_im - phi_two * term_im
    term_re, term_im = columns_forward(receive_one(3))
    state_re = kept_re + phi_two * term_re
    state_im = kept_im + phi_two * term_im

    flow = columns_inverse(cosine * state_re + sine * state_im, cosine * state_im - sine * state_re)
    pl.semaphore_wait(ready, 1)
    send_one(flow, 4, after)
    flow = receive_one(4)

    def folded(value):
        total = value[:8]
        for at in range(1, 32):
            total = total + value[8 * at : 8 * at + 8]
        return jnp.sum(total, axis=0, keepdims=True)

    lines = [folded(flow * spectra[at]) for at in range(KRYLOV)]
    lines.append(folded(flow * flow * weight))
    lines.append(jnp.zeros((7, 128), f32))
    sums = jnp.sum(jnp.concatenate(lines, axis=0), axis=1, keepdims=True)
    spot_row = lax.broadcasted_iota(jnp.int32, (16, 128), 0)
    spot_lane = lax.broadcasted_iota(jnp.int32, (16, 128), 1)
    line = jnp.sum(jnp.where(spot_row == spot_lane, sums, 0.0), axis=0, keepdims=True) + gram_sums

    def spread(target, peers_of, own, count, at):
        target[own] = mine[at]

        def send_to(peers):
            for peer in peers:
                pltpu.make_async_remote_copy(
                    src_ref=mine.at[at],
                    dst_ref=target.at[own],
                    send_sem=send_sem.at[6 + at],
                    recv_sem=recv_sem.at[6 + at],
                    device_id=peer,
                    device_id_type=MESH,
                ).start()

        def step_to(step, carry):
            send_to(peers_of(step))
            return carry

        lax.fori_loop(0, 7, step_to, 0)
        send_to(peers_of(7)[:-1])
        return pltpu.make_async_remote_copy(
            src_ref=target.at[pl.ds(0, count - 1)],
            dst_ref=target.at[pl.ds(0, count - 1)],
            send_sem=send_sem.at[6 + at],
            recv_sem=recv_sem.at[6 + at],
            device_id={"seg": other},
            device_id_type=MESH,
        )

    mine[0] = line
    sent_a = spread(sum_a, peers_in_column, place, COLUMN, 0)
    wrapped = rows_inverse(flow) - start
    sent_a.wait_recv()
    mine[1] = jnp.sum(sum_a[...], axis=0)
    sent_b = spread(sum_b, peers_in_plane, 8 * chip_x + chip_z, PLANE, 1)
    sent_b.wait_recv()
    line = jnp.sum(sum_b[...], axis=0) * (1.0 / (SEGS * GRID * GRID))

    lanes = lax.broadcasted_iota(jnp.int32, (1, 128), 1)

    def lane_of(*signed_places):
        value = jnp.zeros((1, 128), f32)
        for sign, at in signed_places:
            value = value + jnp.where(lanes == at, sign * line, 0.0)
        return jnp.sum(value, axis=1, keepdims=True)

    coeffs = [lane_of((1.0, at), (-1.0, 16 + 8 * at + 7)) for at in range(KRYLOV)]
    norm_sq = lane_of((1.0, KRYLOV), (-2.0, KRYLOV - 1), (1.0, 79))
    left = jnp.zeros((1, 128), f32)
    right = jnp.zeros((1, 128), f32)
    for at in range(KRYLOV):
        left = left + jnp.where((lanes >= 16 + 8 * at) & (lanes < 24 + 8 * at), coeffs[at], 0.0)
        right = right + jnp.where((lanes >= 16) & (lanes % 8 == at) & (lanes < 80), coeffs[at], 0.0)
        norm_sq = norm_sq - 2.0 * coeffs[at] * coeffs[at]
    norm_sq = norm_sq + jnp.sum(left * right * line, axis=1, keepdims=True)
    norm = jnp.sqrt(norm_sq)
    column = jnp.where(lanes == KRYLOV, norm, 0.0)
    for at in range(KRYLOV):
        column = jnp.where(lanes == at, coeffs[at], column)
    hess_ref[...] = column
    inverse = 1.0 / norm
    remainder = wrapped
    for at in range(KRYLOV):
        remainder = remainder - coeffs[at] * basis[at].astype(f32)
    out_ref[0] = remainder * inverse

    for at in range(5):
        arrival(ones_out, ones_in, at, at).wait_send()
    arrival(pair_out, pair_in, 0, 5).wait_send()
    sent_a.wait_send()
    sent_b.wait_send()
    count_copy.wait_send()


def per_device(basis, base_grad, step_counts, shift):
    any_space = pl.BlockSpec(memory_space=pl.ANY)
    scalars = pl.BlockSpec(memory_space=pltpu.SMEM)
    f32, bf16 = jnp.float32, jnp.bfloat16
    new_vector, line = pl.pallas_call(
        kernel,
        out_shape=(
            jax.ShapeDtypeStruct((1, ROWS, GRID), f32),
            jax.ShapeDtypeStruct((1, 128), f32),
        ),
        in_specs=[scalars, scalars] + [any_space] * 4,
        out_specs=(pl.BlockSpec(memory_space=pltpu.VMEM),) * 2,
        scratch_shapes=[
            pltpu.VMEM((KRYLOV, ROWS, GRID), bf16),
            pltpu.VMEM((4, ROWS, GRID), bf16),
            pltpu.VMEM(TABLE.shape, bf16),
            pltpu.VMEM((96, 128), f32),
            pltpu.VMEM((2, 1, 128), jnp.int32),
            pltpu.VMEM((5, SPACE, 5, 128), jnp.int32),
            pltpu.VMEM((5, SPACE, 5, 128), jnp.int32),
            pltpu.VMEM((1, SPACE, 10, 128), jnp.int32),
            pltpu.VMEM((1, SPACE, 10, 128), jnp.int32),
            pltpu.VMEM((KRYLOV, 256, 128), f32),
            pltpu.VMEM((2, 1, 128), f32),
            pltpu.VMEM((COLUMN, 1, 128), f32),
            pltpu.VMEM((PLANE, 1, 128), f32),
            pltpu.SemaphoreType.DMA((4,)),
            pltpu.SemaphoreType.DMA((9,)),
            pltpu.SemaphoreType.DMA((9,)),
            pltpu.SemaphoreType.REGULAR,
            pltpu.SemaphoreType.REGULAR,
        ],
        compiler_params=pltpu.CompilerParams(
            collective_id=0, has_side_effects=True, vmem_limit_bytes=54976 * 1024
        ),
    )(
        step_counts,
        shift,
        basis[0],
        base_grad.reshape(4, ROWS, GRID),
        jnp.asarray(TABLE),
        jnp.asarray(TWIST),
    )
    return new_vector, line[0, : KRYLOV + 1]


def solution(mesh):
    in_specs = (P("seg", None, "space", None), P("seg", None, None, "space", None), P("seg"), P())
    out_specs = (P("seg", "space", None), P())
    return jax.shard_map(
        per_device, mesh=mesh, in_specs=in_specs, out_specs=out_specs, check_vma=False
    )
```

```python
import math

import jax
import jax.numpy as jnp
import ml_dtypes
import numpy as np
from jax import lax
from jax.experimental import pallas as pl
from jax.experimental.pallas import tpu as pltpu
from jax.sharding import PartitionSpec as P

MESH = pl.DeviceIdType.MESH
GRID = 1024
SPACE = 32
SEGS = 16
KRYLOV = 8
PLANE = 32
COLUMN = 16
ROWS = GRID // SPACE
HALF = math.sqrt(0.5)


def make_tables():
    tabs = {}
    small = np.arange(128)
    full = np.arange(256)
    short = np.arange(32)

    def by_owner(real, imag):
        return np.concatenate([real, imag], axis=1)

    def owner_rows(real, imag):
        return np.concatenate([real, imag], axis=0)

    def swapped(table):
        return np.concatenate([table[128:], -table[:128]], axis=0)

    angle = 2 * np.pi / 256 * ((full[:, None] * small[None, :]) % 256)
    real, imag = np.cos(angle), -np.sin(angle)
    imag[:, 0] = (-1.0) ** full
    tabs["A0"] = by_owner(real, imag)
    real, imag = 2 * np.cos(angle.T), -2 * np.sin(angle.T)
    real[0], imag[0] = 1.0, (-1.0) ** full
    tabs["B0"] = owner_rows(real, imag) / GRID
    angle = 2 * np.pi / 128 * ((small[:, None] * small[None, :]) % 128)
    cos, sin = np.cos(angle), np.sin(angle)
    tabs["A1"] = np.concatenate([by_owner(cos, -sin), by_owner(sin, cos)], 0)
    real = np.concatenate([cos, sin], 1)
    imag = np.concatenate([-sin, cos], 1)
    tabs["B1"] = owner_rows(real, imag) * 2 / GRID
    tabs["D0"] = swapped(tabs["B0"])
    tabs["D1"] = swapped(tabs["B1"])
    angle = 2 * np.pi / 32 * ((short[:, None] * short[None, :]) % 32)
    cos, sin = np.cos(angle), np.sin(angle)
    table = np.zeros((2, 5, 32, 2, 32, 4))
    for low in range(4):
        table[0, low, :, 0, :, low] = cos
        table[0, low, :, 1, :, low] = sin
        table[1, low, :, 0, :, low] = -sin
        table[1, low, :, 1, :, low] = cos
    table[0, 4, :, 1, :, 0] = cos
    table[1, 4, :, 1, :, 0] = -sin
    tabs["L1"] = table.reshape(320, 256)
    table = np.zeros((2, 32, 4, 2, 4, 32))
    for low in range(4):
        table[0, :, low, 0, low, :] = cos
        table[0, :, low, 1, low, :] = -sin
        table[1, :, low, 0, low, :] = sin
        table[1, :, low, 1, low, :] = cos
    tabs["M1"] = table.reshape(256, 256) / GRID
    for name, sign in (("L2", 1.0), ("M2", -1.0)):
        table = np.zeros((2, 4, 32, 2, 4, 32))
        for slot in range(4):
            table[0, slot, :, 0, slot, :] = cos
            table[0, slot, :, 1, slot, :] = -sign * sin
            table[1, slot, :, 0, slot, :] = sign * sin
            table[1, slot, :, 1, slot, :] = cos
        tabs[name] = table.reshape(256, 256)
    return tabs


def make_constants():
    offsets, parts, at = {}, [], 0
    for name, table in make_tables().items():
        table = table.astype(np.float32)
        high = table.astype(ml_dtypes.bfloat16)
        low = (table - high.astype(np.float32)).astype(ml_dtypes.bfloat16)
        count = table.shape[0]
        offsets[name] = (at, count)
        parts += [high, low]
        at += 2 * count
    small = np.arange(128)
    short = np.arange(32)
    twist = np.zeros((1024, 128))
    angle = 2 * np.pi / GRID * ((np.arange(1, 4)[:, None] * small[None, :]) % GRID)
    twist[0:3], twist[8:11] = np.cos(angle), np.sin(angle)
    angle = 2 * np.pi / GRID * ((short[:, None] * short[None, :]) % GRID)
    twist[16:48] = np.tile(np.cos(angle), (1, 4))
    twist[48:80] = np.tile(np.sin(angle), (1, 4))
    for slot in range(4):
        freq = 4 * small if slot == 0 else slot + 8 * small
        freq = np.where(freq < GRID // 2, freq, freq - GRID) * (8.0 / GRID)
        twist[80 + slot] = freq
    return offsets, np.concatenate(parts, 0), twist.astype(np.float32)


OFFSETS, TABLE, TWIST = make_constants()


def dot(left, right):
    return jnp.dot(left, right, preferred_element_type=jnp.float32)


def halves(value):
    high = value.astype(jnp.bfloat16)
    return high, (value - high.astype(jnp.float32)).astype(jnp.bfloat16)


def phi_triple(scaled):
    small = jnp.abs(scaled) < 0.5
    safe = jnp.where(small, jnp.ones_like(scaled), scaled)
    inverse = 1.0 / safe
    growth = jnp.exp(safe) - 1.0
    first_phi = growth * inverse
    second_phi = (first_phi - 1.0) * inverse
    series_one = jnp.zeros_like(scaled)
    series_two = jnp.zeros_like(scaled)
    for power in range(10, -1, -1):
        fact_one = float(math.factorial(power + 1))
        series_one = series_one * scaled + 1.0 / fact_one
        series_two = series_two * scaled + 1.0 / (fact_one * (power + 2))
    return (
        jnp.exp(scaled),
        jnp.where(small, series_one, first_phi),
        jnp.where(small, series_two, second_phi),
    )


def kernel(
    steps_ref, shift_ref, basis_hbm, grad_hbm, table_hbm, twist_hbm,
    out_ref, hess_ref,
    basis, grad, table, twist, counts,
    ones_out, ones_in, pair_out, pair_in, spectra,
    mine, sum_a, sum_b,
    local_sem, send_sem, recv_sem, ready, plane,
):
    seg = lax.axis_index("seg")
    me = lax.axis_index("space")
    other = seg + 2 - 4 * (lax.rem(seg, 4) // 2)
    half, place = me // 16, lax.rem(me, 16)
    column_y, core = place // 2, lax.rem(place, 2)
    chip_x, chip_z = seg // 4, lax.rem(seg, 4) + 4 * half
    f32 = jnp.float32

    loads = [
        pltpu.make_async_copy(source, target, local_sem.at[at])
        for at, (source, target) in enumerate(
            ((basis_hbm, basis), (twist_hbm.at[pl.ds(0, 96)], twist), (table_hbm, table), (grad_hbm, grad))
        )
    ]
    before = lax.rem(seg + SEGS - 1, SEGS)
    before = before + 2 - 4 * (lax.rem(before, 4) // 2)
    after = lax.rem(other + 1, SEGS)

    barrier = pltpu.get_barrier_semaphore()

    def far_first(step, size):
        away = (step + 1) // 2
        return lax.rem(size + size // 2 + away * (1 - 2 * lax.rem(step, 2)), size)

    def peers_in_space(step):
        chip_y = 2 * lax.rem(column_y + far_first(step, 8), 8)
        return [16 * upper + chip_y + peer_core for upper in (0, 1) for peer_core in (1 - core, core)]

    def peers_in_plane(step):
        peer_z = lax.rem(chip_z + far_first(step, 8), 8)
        inner, upper = lax.rem(peer_z, 4), 16 * (peer_z // 4) + place
        return [
            {"seg": 4 * lax.rem(chip_x + away, 4) + inner, "space": upper} for away in (2, 1, 3, 0)
        ]

    def peers_in_column(step):
        chip_y = 16 * half + 2 * lax.rem(column_y + far_first(step, 8), 8)
        return [{"space": chip_y + peer_core} for peer_core in (1 - core, core)]

    def greet_space(step, carry):
        for peer in peers_in_space(step):
            pl.semaphore_signal(
                barrier, inc=1, device_id={"seg": other, "space": peer}, device_id_type=MESH
            )
        return carry

    def line_x(step):
        return {"seg": 4 * lax.rem(chip_x + far_first(step, 4), 4) + lax.rem(seg, 4)}

    def greet_x(step, carry):
        pl.semaphore_signal(barrier, inc=1, device_id=line_x(step), device_id_type=MESH)
        return carry

    def greet_z(step, carry):
        peer_z = lax.rem(chip_z + far_first(step, 8), 8)
        peer = {"seg": 4 * chip_x + lax.rem(peer_z, 4), "space": 16 * (peer_z // 4) + place}
        pl.semaphore_signal(barrier, inc=1, device_id=peer, device_id_type=MESH)
        return carry

    def tell_x(step, carry):
        pl.semaphore_signal(plane, inc=1, device_id=line_x(step), device_id_type=MESH)
        return carry

    lax.fori_loop(0, SPACE // 4, greet_space, 0)
    lax.fori_loop(0, 7, greet_z, 0)
    lax.fori_loop(0, 3, greet_x, 0)
    for load in loads:
        load.start()

    def const(name):
        at, count = OFFSETS[name]
        return table[at : at + count, :], table[at + count : at + 2 * count, :]

    def const_left(name, value):
        high, low = halves(value)
        table_high, table_low = const(name)
        both = dot(table_high, jnp.concatenate([high, low], axis=1))
        return both[:, :128] + both[:, 128:] + dot(table_low, high)

    def const_right(value, name):
        high, low = halves(value)
        table_high, table_low = const(name)
        return dot(
            jnp.concatenate([high, high, low], axis=1),
            jnp.concatenate([table_high, table_low, table_high], axis=0),
        )

    def coded(field):
        real, imag = field[:128], field[128:]
        top = jnp.max(jnp.maximum(jnp.abs(real), jnp.abs(imag)), axis=0, keepdims=True)
        level = jnp.ceil(256.0 * jnp.log2(jnp.maximum(top, 1e-30))).astype(jnp.int32) + 1
        scale = jnp.exp2(15.0 - level.astype(f32) * (1.0 / 256.0))
        high = jnp.floor(real * scale + 0.5).astype(jnp.int32)
        low = jnp.floor(imag * scale + 0.5).astype(jnp.int32)
        return (high << 16) | (low & 0xFFFF), level

    def pack(fields, source, at):
        count = len(fields)
        for which, field in enumerate(fields):
            words, level = coded(field)
            for peer in range(SPACE):
                source[at, peer, 4 * which : 4 * which + 4, :] = words[4 * peer : 4 * peer + 4]
            row = 4 * count + which
            source[at, :, row : row + 1, :] = jnp.broadcast_to(level.reshape(1, 1, 128), (SPACE, 1, 128))

    def send(source, target, at, sem, to_seg):
        def step_to(step, carry):
            for peer in peers_in_space(step):
                pltpu.make_async_remote_copy(
                    src_ref=source.at[at, peer],
                    dst_ref=target.at[at, me],
                    send_sem=send_sem.at[sem],
                    recv_sem=recv_sem.at[sem],
                    device_id={"seg": to_seg, "space": peer},
                    device_id_type=MESH,
                ).start()
            return carry

        lax.fori_loop(0, SPACE // 4, step_to, 0)

    def arrival(source, target, at, sem):
        return pltpu.make_async_remote_copy(
            src_ref=source.at[at],
            dst_ref=target.at[at],
            send_sem=send_sem.at[sem],
            recv_sem=recv_sem.at[sem],
            device_id={"space": me},
            device_id_type=MESH,
        )

    def received(target, at, count):
        fields = []
        for which in range(count):
            rows = [target[at, peer, 4 * which : 4 * which + 4, :] for peer in range(SPACE)]
            words = jnp.concatenate(rows, axis=0)
            row = 4 * count + which
            levels = [
                jnp.broadcast_to(target[at, peer, row : row + 1, :], (4, 128)) for peer in range(SPACE)
            ]
            scale = jnp.exp2(jnp.concatenate(levels, axis=0).astype(f32) * (1.0 / 256.0) - 15.0)
            real = (words >> 16).astype(f32) * scale
            imag = ((words << 16) >> 16).astype(f32) * scale
            fields.append(jnp.concatenate([real, imag], axis=0))
        return fields

    def send_one(field, at, to_seg):
        pack([field], ones_out, at)
        send(ones_out, ones_in, at, at, to_seg)

    def receive_one(at):
        arrival(ones_out, ones_in, at, at).wait_recv()
        return received(ones_in, at, 1)[0]

    def basis_spectra(at):
        for index in (2 * at, 2 * at + 1):
            if index == KRYLOV - 1:
                spectra[index] = weight * start_spectrum
            else:
                zero, rest = row_spectrum(basis[index].astype(f32))
                spectra[index] = weight * jnp.concatenate([zero, rest], axis=0).T

    def row_spectrum(field):
        group = [field[:, 128 * at : 128 * at + 128] for at in range(8)]
        plus = [group[at] + group[at + 4] for at in range(4)]
        minus = [group[at] - group[at + 4] for at in range(4)]
        zero = jnp.concatenate([plus[0] + plus[2], plus[1] + plus[3]], axis=1)
        inner = HALF * (minus[1] - minus[3])
        outer = HALF * (minus[1] + minus[3])
        pairs = (
            (minus[0] + inner, -(minus[2] + outer)),
            (plus[0] - plus[2], plus[3] - plus[1]),
            (minus[0] - inner, minus[2] - outer),
        )
        rest = []
        for at, (real, imag) in enumerate(pairs):
            cos, sin = twist[at : at + 1, :], twist[8 + at : 9 + at, :]
            rest.append(
                jnp.concatenate([real * cos + imag * sin, imag * cos - real * sin], axis=1)
            )
        return const_right(zero, "A0"), const_right(jnp.concatenate(rest, axis=0), "A1")

    def row_field(zero, rest):
        turned = []
        for at in range(3):
            real, imag = rest[32 * at : 32 * at + 32, :128], rest[32 * at : 32 * at + 32, 128:]
            cos, sin = twist[at : at + 1, :], twist[8 + at : 9 + at, :]
            turned.append((real * cos - imag * sin, real * sin + imag * cos))
        (re1, im1), (re2, im2), (re3, im3) = turned
        even, odd = zero[:, :128], zero[:, 128:]
        sums = (even + re2, odd - im2, even - re2, odd + im2)
        differences = (
            re1 + re3,
            HALF * ((re1 - im1) - (re3 + im3)),
            im3 - im1,
            HALF * ((re3 - im3) - (re1 + im1)),
        )
        pieces = [sums[at] + differences[at] for at in range(4)]
        pieces += [sums[at] - differences[at] for at in range(4)]
        return jnp.concatenate(pieces, axis=1)

    def rows_forward(field):
        zero, rest = row_spectrum(field)
        return jnp.concatenate([zero, rest], axis=0).T

    def rows_inverse(spectrum):
        turned = spectrum.T
        return row_field(const_right(turned[:32], "B0"), const_right(turned[32:], "B1"))

    def stacked(value):
        return jnp.concatenate([value] * 5, axis=0)

    lane = lax.broadcasted_iota(jnp.int32, (160, 128), 1)
    row = lax.broadcasted_iota(jnp.int32, (160, 128), 0)
    anchor = jnp.where((lane[:32] < 32) & (me == 0), 1.0, 0.0).astype(f32)

    def columns_forward(received):
        value = const_left("L1", received)
        real, imag = value[:160], value[160:]
        real = jnp.concatenate([real[:32] + anchor * imag[128:], real[32:]], axis=0)
        imag = jnp.concatenate([imag[:32] - anchor * value[128:160], imag[32:]], axis=0)
        cos, sin = stacked(twist[16:48, :]), stacked(twist[48:80, :])
        turned = jnp.concatenate([real * cos + imag * sin, imag * cos - real * sin], axis=1)
        value = const_right(turned, "L2")
        return value[:, :128], value[:, 128:]

    def columns_inverse(real, imag):
        value = const_right(jnp.concatenate([real, imag], axis=1), "M2")
        real, imag = value[:, :128], value[:, 128:]
        cos, sin = stacked(twist[16:48, :]), stacked(twist[48:80, :])
        real, imag = real * cos - imag * sin, real * sin + imag * cos
        value = jnp.concatenate(
            [real[:32] - anchor * imag[128:], real[32:128], imag[:32] + anchor * real[128:], imag[32:128]],
            axis=0,
        )
        return const_left("M1", value)

    pair_row = lax.broadcasted_iota(jnp.int32, (256, 128), 0)
    pair_lane = lax.broadcasted_iota(jnp.int32, (256, 128), 1)
    alone = (pair_row % 128 == 0) & (pair_lane < 32)
    weight = jnp.where(alone, 1.0 / GRID, 2.0 / GRID).astype(f32)

    loads[0].wait()
    loads[1].wait()
    loads[2].wait()
    start = basis[KRYLOV - 1].astype(f32)
    zero, rest = row_spectrum(start)
    start_spectrum = jnp.concatenate([zero, rest], axis=0).T
    pack([start_spectrum], ones_out, 0)
    pl.semaphore_wait(barrier, SPACE + 10)
    send(ones_out, ones_in, 0, 0, other)
    lax.fori_loop(0, 3, tell_x, 0)
    counts[0] = jnp.full((1, 128), steps_ref[0], jnp.int32)
    count_copy = pltpu.make_async_remote_copy(
        src_ref=counts.at[0],
        dst_ref=counts.at[1],
        send_sem=send_sem.at[8],
        recv_sem=recv_sem.at[8],
        device_id={"seg": other},
        device_id_type=MESH,
    )
    count_copy.start()
    basis_spectra(0)

    waves = [
        jnp.concatenate([twist[80 + at : 81 + at, :]] * 2, axis=1)
        for at in range(4)
    ]
    lifted = jnp.concatenate([rest[32 * at : 32 * at + 32] * waves[at + 1] for at in range(3)], axis=0)
    grad_y = row_field(const_right(zero * waves[0], "D0"), const_right(lifted, "D1"))

    slot = lane // 32
    low = row // 32
    freq_x = row % 32 + 32 * (lane % 32)
    base = 4 * me + low
    freq_y = jnp.where(low == 4, GRID // 2, jnp.where(slot == 0, 4 * base, slot + 8 * base))
    signed_x = jnp.where(freq_x < GRID // 2, freq_x, freq_x - GRID)
    signed_y = jnp.where(freq_y < GRID // 2, freq_y, freq_y - GRID)
    wave_x = signed_x.astype(f32) * (8.0 / GRID)
    wave_y = signed_y.astype(f32) * (8.0 / GRID)
    deriv_x = jnp.where(signed_x == -(GRID // 2), 0.0, wave_x)
    deriv_y = jnp.where(signed_y == -(GRID // 2), 0.0, wave_y)
    squared = wave_x * wave_x + wave_y * wave_y
    count_copy.wait_recv()
    step_size = 0.01 * counts[1].astype(f32)
    decay, phi_one, phi_two = phi_triple((squared - squared * squared) * step_size)
    phi_one = step_size * phi_one
    phi_two = step_size * phi_two

    state_re, state_im = columns_forward(receive_one(0))

    send_one(columns_inverse(-deriv_x * state_im, deriv_x * state_re), 1, other)
    basis_spectra(1)
    loads[3].wait()
    part_y = grad[1].astype(f32) * grad_y
    part_x = -grad[0].astype(f32)
    slope = receive_one(1)
    pl.semaphore_wait(plane, 3)
    pl.semaphore_signal(ready, inc=1, device_id={"seg": before}, device_id_type=MESH)
    term = part_x * rows_inverse(slope) - part_y

    send_one(rows_forward(term), 2, other)
    basis_spectra(2)
    flat = basis[...].reshape(KRYLOV * ROWS, GRID)
    gram = lax.dot_general(flat, flat, (((1,), (1,)), ((), ())), preferred_element_type=f32)
    gram_row = lax.broadcasted_iota(jnp.int32, (256, 256), 0)
    gram_lane = lax.broadcasted_iota(jnp.int32, (256, 256), 1)
    gram = jnp.where(gram_row % 32 == gram_lane % 32, gram, 0.0)
    gram = jnp.concatenate(
        [jnp.sum(gram[32 * at : 32 * at + 32], axis=0, keepdims=True) for at in range(8)], axis=0
    )
    spot_row = lax.broadcasted_iota(jnp.int32, (8, 128), 0)
    spot_lane = lax.broadcasted_iota(jnp.int32, (8, 128), 1)
    gram_sums = jnp.zeros((8, 128), f32)
    for at in range(8):
        part = jnp.sum(jnp.where(gram_lane[:8] // 32 == at, gram, 0.0), axis=1, keepdims=True)
        gram_sums = gram_sums + jnp.where(spot_lane == 16 + 8 * spot_row + at, part, 0.0)
    gram_sums = jnp.sum(gram_sums, axis=0, keepdims=True)
    term_re, term_im = columns_forward(receive_one(2))
    middle_re = decay * state_re + phi_one * term_re
    middle_im = decay * state_im + phi_one * term_im

    toward_x = columns_inverse(-deriv_x * middle_im, deriv_x * middle_re)
    toward_y = columns_inverse(-deriv_y * middle_im, deriv_y * middle_re)
    pack([toward_x, toward_y], pair_out, 0)
    send(pair_out, pair_in, 0, 5, other)
    basis_spectra(3)
    offset = (freq_x * shift_ref[0] + freq_y * shift_ref[1]) & (GRID - 1)
    angle = (2.0 * math.pi / GRID) * offset.astype(f32)
    is_last = other == SEGS - 1
    cosine = jnp.where(is_last, jnp.cos(angle), 1.0)
    sine = jnp.where(is_last, jnp.sin(angle), 0.0)
    arrival(pair_out, pair_in, 0, 5).wait_recv()
    got_x, got_y = received(pair_in, 0, 2)
    term = -(grad[2].astype(f32) * rows_inverse(got_x) + grad[3].astype(f32) * rows_inverse(got_y))

    send_one(rows_forward(term), 3, other)
    kept_re = middle_re - phi_two * term_re
    kept_im = middle_im - phi_two * term_im
    term_re, term_im = columns_forward(receive_one(3))
    state_re = kept_re + phi_two * term_re
    state_im = kept_im + phi_two * term_im

    flow = columns_inverse(cosine * state_re + sine * state_im, cosine * state_im - sine * state_re)
    pl.semaphore_wait(ready, 1)
    send_one(flow, 4, after)
    flow = receive_one(4)

    def folded(value):
        total = value[:8]
        for at in range(1, 32):
            total = total + value[8 * at : 8 * at + 8]
        return jnp.sum(total, axis=0, keepdims=True)

    lines = [folded(flow * spectra[at]) for at in range(KRYLOV)]
    lines.append(folded(flow * flow * weight))
    lines.append(jnp.zeros((7, 128), f32))
    sums = jnp.sum(jnp.concatenate(lines, axis=0), axis=1, keepdims=True)
    spot_row = lax.broadcasted_iota(jnp.int32, (16, 128), 0)
    spot_lane = lax.broadcasted_iota(jnp.int32, (16, 128), 1)
    line = jnp.sum(jnp.where(spot_row == spot_lane, sums, 0.0), axis=0, keepdims=True) + gram_sums

    def spread(target, peers_of, own, count, at):
        target[own] = mine[at]

        def send_to(peers):
            for peer in peers:
                pltpu.make_async_remote_copy(
                    src_ref=mine.at[at],
                    dst_ref=target.at[own],
                    send_sem=send_sem.at[6 + at],
                    recv_sem=recv_sem.at[6 + at],
                    device_id=peer,
                    device_id_type=MESH,
                ).start()

        def step_to(step, carry):
            send_to(peers_of(step))
            return carry

        lax.fori_loop(0, 7, step_to, 0)
        send_to(peers_of(7)[:-1])
        return pltpu.make_async_remote_copy(
            src_ref=target.at[pl.ds(0, count - 1)],
            dst_ref=target.at[pl.ds(0, count - 1)],
            send_sem=send_sem.at[6 + at],
            recv_sem=recv_sem.at[6 + at],
            device_id={"seg": other},
            device_id_type=MESH,
        )

    mine[0] = line
    sent_a = spread(sum_a, peers_in_column, place, COLUMN, 0)
    wrapped = rows_inverse(flow) - start
    sent_a.wait_recv()
    mine[1] = jnp.sum(sum_a[...], axis=0)
    sent_b = spread(sum_b, peers_in_plane, 8 * chip_x + chip_z, PLANE, 1)
    sent_b.wait_recv()
    line = jnp.sum(sum_b[...], axis=0) * (1.0 / (SEGS * GRID * GRID))

    lanes = lax.broadcasted_iota(jnp.int32, (1, 128), 1)

    def lane_of(*signed_places):
        value = jnp.zeros((1, 128), f32)
        for sign, at in signed_places:
            value = value + jnp.where(lanes == at, sign * line, 0.0)
        return jnp.sum(value, axis=1, keepdims=True)

    coeffs = [lane_of((1.0, at), (-1.0, 16 + 8 * at + 7)) for at in range(KRYLOV)]
    norm_sq = lane_of((1.0, KRYLOV), (-2.0, KRYLOV - 1), (1.0, 79))
    left = jnp.zeros((1, 128), f32)
    right = jnp.zeros((1, 128), f32)
    for at in range(KRYLOV):
        left = left + jnp.where((lanes >= 16 + 8 * at) & (lanes < 24 + 8 * at), coeffs[at], 0.0)
        right = right + jnp.where((lanes >= 16) & (lanes % 8 == at) & (lanes < 80), coeffs[at], 0.0)
        norm_sq = norm_sq - 2.0 * coeffs[at] * coeffs[at]
    norm_sq = norm_sq + jnp.sum(left * right * line, axis=1, keepdims=True)
    norm = jnp.sqrt(norm_sq)
    column = jnp.where(lanes == KRYLOV, norm, 0.0)
    for at in range(KRYLOV):
        column = jnp.where(lanes == at, coeffs[at], column)
    hess_ref[...] = column
    inverse = 1.0 / norm
    remainder = wrapped
    for at in range(KRYLOV):
        remainder = remainder - coeffs[at] * basis[at].astype(f32)
    out_ref[0] = remainder * inverse

    for at in range(5):
        arrival(ones_out, ones_in, at, at).wait_send()
    arrival(pair_out, pair_in, 0, 5).wait_send()
    sent_a.wait_send()
    sent_b.wait_send()
    count_copy.wait_send()


def per_device(basis, base_grad, step_counts, shift):
    any_space = pl.BlockSpec(memory_space=pl.ANY)
    scalars = pl.BlockSpec(memory_space=pltpu.SMEM)
    f32, bf16 = jnp.float32, jnp.bfloat16
    new_vector, line = pl.pallas_call(
        kernel,
        out_shape=(
            jax.ShapeDtypeStruct((1, ROWS, GRID), f32),
            jax.ShapeDtypeStruct((1, 128), f32),
        ),
        grid_spec=pltpu.PrefetchScalarGridSpec(
            num_scalar_prefetch=2,
            grid=(),
            in_specs=[any_space] * 4,
            out_specs=(pl.BlockSpec(memory_space=pltpu.VMEM),) * 2,
            scratch_shapes=[
            pltpu.VMEM((KRYLOV, ROWS, GRID), bf16),
            pltpu.VMEM((4, ROWS, GRID), bf16),
            pltpu.VMEM(TABLE.shape, bf16),
            pltpu.VMEM((96, 128), f32),
            pltpu.VMEM((2, 1, 128), jnp.int32),
            pltpu.VMEM((5, SPACE, 5, 128), jnp.int32),
            pltpu.VMEM((5, SPACE, 5, 128), jnp.int32),
            pltpu.VMEM((1, SPACE, 10, 128), jnp.int32),
            pltpu.VMEM((1, SPACE, 10, 128), jnp.int32),
            pltpu.VMEM((KRYLOV, 256, 128), f32),
            pltpu.VMEM((2, 1, 128), f32),
            pltpu.VMEM((COLUMN, 1, 128), f32),
            pltpu.VMEM((PLANE, 1, 128), f32),
            pltpu.SemaphoreType.DMA((4,)),
            pltpu.SemaphoreType.DMA((9,)),
            pltpu.SemaphoreType.DMA((9,)),
            pltpu.SemaphoreType.REGULAR,
            pltpu.SemaphoreType.REGULAR,
        ],
        ),
        compiler_params=pltpu.CompilerParams(
            collective_id=0, has_side_effects=True, vmem_limit_bytes=54976 * 1024
        ),
    )(
        step_counts,
        shift,
        basis[0],
        base_grad.reshape(4, ROWS, GRID),
        jnp.asarray(TABLE),
        jnp.asarray(TWIST),
    )
    return new_vector, line[0, : KRYLOV + 1]


def solution(mesh):
    in_specs = (P("seg", None, "space", None), P("seg", None, None, "space", None), P("seg"), P())
    out_specs = (P("seg", "space", None), P())
    return jax.shard_map(
        per_device, mesh=mesh, in_specs=in_specs, out_specs=out_specs, check_vma=False
    )
```

```python
import math

import jax
import jax.numpy as jnp
import ml_dtypes
import numpy as np
from jax import lax
from jax.experimental import pallas as pl
from jax.experimental.pallas import tpu as pltpu
from jax.sharding import PartitionSpec as P

MESH = pl.DeviceIdType.MESH
GRID = 1024
SPACE = 32
SEGS = 16
KRYLOV = 8
PLANE = 32
COLUMN = 16
ROWS = GRID // SPACE
HALF = math.sqrt(0.5)


def make_tables():
    tabs = {}
    small = np.arange(128)
    full = np.arange(256)
    short = np.arange(32)

    def by_owner(real, imag):
        return np.concatenate([real, imag], axis=1)

    def owner_rows(real, imag):
        return np.concatenate([real, imag], axis=0)

    def swapped(table):
        return np.concatenate([table[128:], -table[:128]], axis=0)

    angle = 2 * np.pi / 256 * ((full[:, None] * small[None, :]) % 256)
    real, imag = np.cos(angle), -np.sin(angle)
    imag[:, 0] = (-1.0) ** full
    tabs["A0"] = by_owner(real, imag)
    real, imag = 2 * np.cos(angle.T), -2 * np.sin(angle.T)
    real[0], imag[0] = 1.0, (-1.0) ** full
    tabs["B0"] = owner_rows(real, imag) / GRID
    angle = 2 * np.pi / 128 * ((small[:, None] * small[None, :]) % 128)
    cos, sin = np.cos(angle), np.sin(angle)
    tabs["A1"] = np.concatenate([by_owner(cos, -sin), by_owner(sin, cos)], 0)
    real = np.concatenate([cos, sin], 1)
    imag = np.concatenate([-sin, cos], 1)
    tabs["B1"] = owner_rows(real, imag) * 2 / GRID
    tabs["D0"] = swapped(tabs["B0"])
    tabs["D1"] = swapped(tabs["B1"])
    angle = 2 * np.pi / 32 * ((short[:, None] * short[None, :]) % 32)
    cos, sin = np.cos(angle), np.sin(angle)
    table = np.zeros((2, 5, 32, 2, 32, 4))
    for low in range(4):
        table[0, low, :, 0, :, low] = cos
        table[0, low, :, 1, :, low] = sin
        table[1, low, :, 0, :, low] = -sin
        table[1, low, :, 1, :, low] = cos
    table[0, 4, :, 1, :, 0] = cos
    table[1, 4, :, 1, :, 0] = -sin
    tabs["L1"] = table.reshape(320, 256)
    table = np.zeros((2, 32, 4, 2, 4, 32))
    for low in range(4):
        table[0, :, low, 0, low, :] = cos
        table[0, :, low, 1, low, :] = -sin
        table[1, :, low, 0, low, :] = sin
        table[1, :, low, 1, low, :] = cos
    tabs["M1"] = table.reshape(256, 256) / GRID
    for name, sign in (("L2", 1.0), ("M2", -1.0)):
        table = np.zeros((2, 4, 32, 2, 4, 32))
        for slot in range(4):
            table[0, slot, :, 0, slot, :] = cos
            table[0, slot, :, 1, slot, :] = -sign * sin
            table[1, slot, :, 0, slot, :] = sign * sin
            table[1, slot, :, 1, slot, :] = cos
        tabs[name] = table.reshape(256, 256)
    return tabs


def make_constants():
    offsets, parts, at = {}, [], 0
    for name, table in make_tables().items():
        table = table.astype(np.float32)
        high = table.astype(ml_dtypes.bfloat16)
        low = (table - high.astype(np.float32)).astype(ml_dtypes.bfloat16)
        count = table.shape[0]
        offsets[name] = (at, count)
        parts += [high, low]
        at += 2 * count
    small = np.arange(128)
    short = np.arange(32)
    twist = np.zeros((1024, 128))
    angle = 2 * np.pi / GRID * ((np.arange(1, 4)[:, None] * small[None, :]) % GRID)
    twist[0:3], twist[8:11] = np.cos(angle), np.sin(angle)
    angle = 2 * np.pi / GRID * ((short[:, None] * short[None, :]) % GRID)
    twist[16:48] = np.tile(np.cos(angle), (1, 4))
    twist[48:80] = np.tile(np.sin(angle), (1, 4))
    for slot in range(4):
        freq = 4 * small if slot == 0 else slot + 8 * small
        freq = np.where(freq < GRID // 2, freq, freq - GRID) * (8.0 / GRID)
        twist[80 + slot] = freq
    return offsets, np.concatenate(parts, 0), twist.astype(np.float32)


OFFSETS, TABLE, TWIST = make_constants()


def dot(left, right):
    return jnp.dot(left, right, preferred_element_type=jnp.float32)


def halves(value):
    high = value.astype(jnp.bfloat16)
    return high, (value - high.astype(jnp.float32)).astype(jnp.bfloat16)


def phi_triple(scaled):
    small = jnp.abs(scaled) < 0.5
    safe = jnp.where(small, jnp.ones_like(scaled), scaled)
    inverse = 1.0 / safe
    growth = jnp.exp(safe) - 1.0
    first_phi = growth * inverse
    second_phi = (first_phi - 1.0) * inverse
    series_one = jnp.zeros_like(scaled)
    series_two = jnp.zeros_like(scaled)
    for power in range(10, -1, -1):
        fact_one = float(math.factorial(power + 1))
        series_one = series_one * scaled + 1.0 / fact_one
        series_two = series_two * scaled + 1.0 / (fact_one * (power + 2))
    return (
        jnp.exp(scaled),
        jnp.where(small, series_one, first_phi),
        jnp.where(small, series_two, second_phi),
    )


def kernel(
    steps_ref, shift_ref, basis_hbm, grad_hbm, table_hbm, twist_hbm,
    out_ref, hess_ref,
    basis, grad, table, twist, counts,
    ones_out, ones_in, pair_out, pair_in, spectra,
    mine, sum_a, sum_b,
    local_sem, send_sem, recv_sem, ready, plane,
):
    seg = lax.axis_index("seg")
    me = lax.axis_index("space")
    other = seg + 2 - 4 * (lax.rem(seg, 4) // 2)
    half, place = me // 16, lax.rem(me, 16)
    column_y, core = place // 2, lax.rem(place, 2)
    chip_x, chip_z = seg // 4, lax.rem(seg, 4) + 4 * half
    f32 = jnp.float32

    loads = [
        pltpu.make_async_copy(source, target, local_sem.at[at])
        for at, (source, target) in enumerate(
            ((basis_hbm, basis), (twist_hbm.at[pl.ds(0, 96)], twist), (table_hbm, table), (grad_hbm, grad))
        )
    ]
    before = lax.rem(seg + SEGS - 1, SEGS)
    before = before + 2 - 4 * (lax.rem(before, 4) // 2)
    after = lax.rem(other + 1, SEGS)

    barrier = pltpu.get_barrier_semaphore()

    def far_first(step, size):
        away = (step + 1) // 2
        return lax.rem(size + size // 2 + away * (1 - 2 * lax.rem(step, 2)), size)

    def peers_in_space(step):
        chip_y = 2 * lax.rem(column_y + far_first(step, 8), 8)
        return [16 * upper + chip_y + peer_core for upper in (0, 1) for peer_core in (1 - core, core)]

    def peers_in_plane(step):
        peer_z = lax.rem(chip_z + far_first(step, 8), 8)
        inner, upper = lax.rem(peer_z, 4), 16 * (peer_z // 4) + place
        return [
            {"seg": 4 * lax.rem(chip_x + away, 4) + inner, "space": upper} for away in (2, 1, 3, 0)
        ]

    def peers_in_column(step):
        chip_y = 16 * half + 2 * lax.rem(column_y + far_first(step, 8), 8)
        return [{"space": chip_y + peer_core} for peer_core in (1 - core, core)]

    def greet_space(step, carry):
        for peer in peers_in_space(step):
            pl.semaphore_signal(
                barrier, inc=1, device_id={"seg": other, "space": peer}, device_id_type=MESH
            )
        return carry

    def line_x(step):
        return {"seg": 4 * lax.rem(chip_x + far_first(step, 4), 4) + lax.rem(seg, 4)}

    def greet_x(step, carry):
        pl.semaphore_signal(barrier, inc=1, device_id=line_x(step), device_id_type=MESH)
        return carry

    def greet_z(step, carry):
        peer_z = lax.rem(chip_z + far_first(step, 8), 8)
        peer = {"seg": 4 * chip_x + lax.rem(peer_z, 4), "space": 16 * (peer_z // 4) + place}
        pl.semaphore_signal(barrier, inc=1, device_id=peer, device_id_type=MESH)
        return carry

    def tell_x(step, carry):
        pl.semaphore_signal(plane, inc=1, device_id=line_x(step), device_id_type=MESH)
        return carry

    lax.fori_loop(0, SPACE // 4, greet_space, 0, unroll=True)
    lax.fori_loop(0, 7, greet_z, 0, unroll=True)
    lax.fori_loop(0, 3, greet_x, 0, unroll=True)
    for load in loads:
        load.start()

    def const(name):
        at, count = OFFSETS[name]
        return table[at : at + count, :], table[at + count : at + 2 * count, :]

    def const_left(name, value):
        high, low = halves(value)
        table_high, table_low = const(name)
        both = dot(table_high, jnp.concatenate([high, low], axis=1))
        return both[:, :128] + both[:, 128:] + dot(table_low, high)

    def const_right(value, name):
        high, low = halves(value)
        table_high, table_low = const(name)
        return dot(
            jnp.concatenate([high, high, low], axis=1),
            jnp.concatenate([table_high, table_low, table_high], axis=0),
        )

    def coded(field):
        real, imag = field[:128], field[128:]
        top = jnp.max(jnp.maximum(jnp.abs(real), jnp.abs(imag)), axis=0, keepdims=True)
        level = jnp.ceil(256.0 * jnp.log2(jnp.maximum(top, 1e-30))).astype(jnp.int32) + 1
        scale = jnp.exp2(15.0 - level.astype(f32) * (1.0 / 256.0))
        high = jnp.floor(real * scale + 0.5).astype(jnp.int32)
        low = jnp.floor(imag * scale + 0.5).astype(jnp.int32)
        return (high << 16) | (low & 0xFFFF), level

    def pack(fields, source, at):
        count = len(fields)
        for which, field in enumerate(fields):
            words, level = coded(field)
            for peer in range(SPACE):
                source[at, peer, 4 * which : 4 * which + 4, :] = words[4 * peer : 4 * peer + 4]
            row = 4 * count + which
            source[at, :, row : row + 1, :] = jnp.broadcast_to(level.reshape(1, 1, 128), (SPACE, 1, 128))

    def send(source, target, at, sem, to_seg):
        def step_to(step, carry):
            for peer in peers_in_space(step):
                pltpu.make_async_remote_copy(
                    src_ref=source.at[at, peer],
                    dst_ref=target.at[at, me],
                    send_sem=send_sem.at[sem],
                    recv_sem=recv_sem.at[sem],
                    device_id={"seg": to_seg, "space": peer},
                    device_id_type=MESH,
                ).start()
            return carry

        lax.fori_loop(0, SPACE // 4, step_to, 0)

    def arrival(source, target, at, sem):
        return pltpu.make_async_remote_copy(
            src_ref=source.at[at],
            dst_ref=target.at[at],
            send_sem=send_sem.at[sem],
            recv_sem=recv_sem.at[sem],
            device_id={"space": me},
            device_id_type=MESH,
        )

    def received(target, at, count):
        fields = []
        for which in range(count):
            rows = [target[at, peer, 4 * which : 4 * which + 4, :] for peer in range(SPACE)]
            words = jnp.concatenate(rows, axis=0)
            row = 4 * count + which
            levels = [
                jnp.broadcast_to(target[at, peer, row : row + 1, :], (4, 128)) for peer in range(SPACE)
            ]
            scale = jnp.exp2(jnp.concatenate(levels, axis=0).astype(f32) * (1.0 / 256.0) - 15.0)
            real = (words >> 16).astype(f32) * scale
            imag = ((words << 16) >> 16).astype(f32) * scale
            fields.append(jnp.concatenate([real, imag], axis=0))
        return fields

    def send_one(field, at, to_seg):
        pack([field], ones_out, at)
        send(ones_out, ones_in, at, at, to_seg)

    def receive_one(at):
        arrival(ones_out, ones_in, at, at).wait_recv()
        return received(ones_in, at, 1)[0]

    def basis_spectra(at):
        for index in (2 * at, 2 * at + 1):
            if index == KRYLOV - 1:
                spectra[index] = weight * start_spectrum
            else:
                zero, rest = row_spectrum(basis[index].astype(f32))
                spectra[index] = weight * jnp.concatenate([zero, rest], axis=0).T

    def row_spectrum(field):
        group = [field[:, 128 * at : 128 * at + 128] for at in range(8)]
        plus = [group[at] + group[at + 4] for at in range(4)]
        minus = [group[at] - group[at + 4] for at in range(4)]
        zero = jnp.concatenate([plus[0] + plus[2], plus[1] + plus[3]], axis=1)
        inner = HALF * (minus[1] - minus[3])
        outer = HALF * (minus[1] + minus[3])
        pairs = (
            (minus[0] + inner, -(minus[2] + outer)),
            (plus[0] - plus[2], plus[3] - plus[1]),
            (minus[0] - inner, minus[2] - outer),
        )
        rest = []
        for at, (real, imag) in enumerate(pairs):
            cos, sin = twist[at : at + 1, :], twist[8 + at : 9 + at, :]
            rest.append(
                jnp.concatenate([real * cos + imag * sin, imag * cos - real * sin], axis=1)
            )
        return const_right(zero, "A0"), const_right(jnp.concatenate(rest, axis=0), "A1")

    def row_field(zero, rest):
        turned = []
        for at in range(3):
            real, imag = rest[32 * at : 32 * at + 32, :128], rest[32 * at : 32 * at + 32, 128:]
            cos, sin = twist[at : at + 1, :], twist[8 + at : 9 + at, :]
            turned.append((real * cos - imag * sin, real * sin + imag * cos))
        (re1, im1), (re2, im2), (re3, im3) = turned
        even, odd = zero[:, :128], zero[:, 128:]
        sums = (even + re2, odd - im2, even - re2, odd + im2)
        differences = (
            re1 + re3,
            HALF * ((re1 - im1) - (re3 + im3)),
            im3 - im1,
            HALF * ((re3 - im3) - (re1 + im1)),
        )
        pieces = [sums[at] + differences[at] for at in range(4)]
        pieces += [sums[at] - differences[at] for at in range(4)]
        return jnp.concatenate(pieces, axis=1)

    def rows_forward(field):
        zero, rest = row_spectrum(field)
        return jnp.concatenate([zero, rest], axis=0).T

    def rows_inverse(spectrum):
        turned = spectrum.T
        return row_field(const_right(turned[:32], "B0"), const_right(turned[32:], "B1"))

    def stacked(value):
        return jnp.concatenate([value] * 5, axis=0)

    lane = lax.broadcasted_iota(jnp.int32, (160, 128), 1)
    row = lax.broadcasted_iota(jnp.int32, (160, 128), 0)
    anchor = jnp.where((lane[:32] < 32) & (me == 0), 1.0, 0.0).astype(f32)

    def columns_forward(received):
        value = const_left("L1", received)
        real, imag = value[:160], value[160:]
        real = jnp.concatenate([real[:32] + anchor * imag[128:], real[32:]], axis=0)
        imag = jnp.concatenate([imag[:32] - anchor * value[128:160], imag[32:]], axis=0)
        cos, sin = stacked(twist[16:48, :]), stacked(twist[48:80, :])
        turned = jnp.concatenate([real * cos + imag * sin, imag * cos - real * sin], axis=1)
        value = const_right(turned, "L2")
        return value[:, :128], value[:, 128:]

    def columns_inverse(real, imag):
        value = const_right(jnp.concatenate([real, imag], axis=1), "M2")
        real, imag = value[:, :128], value[:, 128:]
        cos, sin = stacked(twist[16:48, :]), stacked(twist[48:80, :])
        real, imag = real * cos - imag * sin, real * sin + imag * cos
        value = jnp.concatenate(
            [real[:32] - anchor * imag[128:], real[32:128], imag[:32] + anchor * real[128:], imag[32:128]],
            axis=0,
        )
        return const_left("M1", value)

    pair_row = lax.broadcasted_iota(jnp.int32, (256, 128), 0)
    pair_lane = lax.broadcasted_iota(jnp.int32, (256, 128), 1)
    alone = (pair_row % 128 == 0) & (pair_lane < 32)
    weight = jnp.where(alone, 1.0 / GRID, 2.0 / GRID).astype(f32)

    loads[0].wait()
    loads[1].wait()
    loads[2].wait()
    start = basis[KRYLOV - 1].astype(f32)
    zero, rest = row_spectrum(start)
    start_spectrum = jnp.concatenate([zero, rest], axis=0).T
    pack([start_spectrum], ones_out, 0)
    pl.semaphore_wait(barrier, SPACE + 10)
    send(ones_out, ones_in, 0, 0, other)
    lax.fori_loop(0, 3, tell_x, 0)
    counts[0] = jnp.full((1, 128), steps_ref[0], jnp.int32)
    count_copy = pltpu.make_async_remote_copy(
        src_ref=counts.at[0],
        dst_ref=counts.at[1],
        send_sem=send_sem.at[8],
        recv_sem=recv_sem.at[8],
        device_id={"seg": other},
        device_id_type=MESH,
    )
    count_copy.start()
    basis_spectra(0)

    waves = [
        jnp.concatenate([twist[80 + at : 81 + at, :]] * 2, axis=1)
        for at in range(4)
    ]
    lifted = jnp.concatenate([rest[32 * at : 32 * at + 32] * waves[at + 1] for at in range(3)], axis=0)
    grad_y = row_field(const_right(zero * waves[0], "D0"), const_right(lifted, "D1"))

    slot = lane // 32
    low = row // 32
    freq_x = row % 32 + 32 * (lane % 32)
    base = 4 * me + low
    freq_y = jnp.where(low == 4, GRID // 2, jnp.where(slot == 0, 4 * base, slot + 8 * base))
    signed_x = jnp.where(freq_x < GRID // 2, freq_x, freq_x - GRID)
    signed_y = jnp.where(freq_y < GRID // 2, freq_y, freq_y - GRID)
    wave_x = signed_x.astype(f32) * (8.0 / GRID)
    wave_y = signed_y.astype(f32) * (8.0 / GRID)
    deriv_x = jnp.where(signed_x == -(GRID // 2), 0.0, wave_x)
    deriv_y = jnp.where(signed_y == -(GRID // 2), 0.0, wave_y)
    squared = wave_x * wave_x + wave_y * wave_y
    count_copy.wait_recv()
    step_size = 0.01 * counts[1].astype(f32)
    decay, phi_one, phi_two = phi_triple((squared - squared * squared) * step_size)
    phi_one = step_size * phi_one
    phi_two = step_size * phi_two

    state_re, state_im = columns_forward(receive_one(0))

    send_one(columns_inverse(-deriv_x * state_im, deriv_x * state_re), 1, other)
    basis_spectra(1)
    loads[3].wait()
    part_y = grad[1].astype(f32) * grad_y
    part_x = -grad[0].astype(f32)
    slope = receive_one(1)
    pl.semaphore_wait(plane, 3)
    pl.semaphore_signal(ready, inc=1, device_id={"seg": before}, device_id_type=MESH)
    term = part_x * rows_inverse(slope) - part_y

    send_one(rows_forward(term), 2, other)
    basis_spectra(2)
    flat = basis[...].reshape(KRYLOV * ROWS, GRID)
    gram = lax.dot_general(flat, flat, (((1,), (1,)), ((), ())), preferred_element_type=f32)
    gram_row = lax.broadcasted_iota(jnp.int32, (256, 256), 0)
    gram_lane = lax.broadcasted_iota(jnp.int32, (256, 256), 1)
    gram = jnp.where(gram_row % 32 == gram_lane % 32, gram, 0.0)
    gram = jnp.concatenate(
        [jnp.sum(gram[32 * at : 32 * at + 32], axis=0, keepdims=True) for at in range(8)], axis=0
    )
    spot_row = lax.broadcasted_iota(jnp.int32, (8, 128), 0)
    spot_lane = lax.broadcasted_iota(jnp.int32, (8, 128), 1)
    gram_sums = jnp.zeros((8, 128), f32)
    for at in range(8):
        part = jnp.sum(jnp.where(gram_lane[:8] // 32 == at, gram, 0.0), axis=1, keepdims=True)
        gram_sums = gram_sums + jnp.where(spot_lane == 16 + 8 * spot_row + at, part, 0.0)
    gram_sums = jnp.sum(gram_sums, axis=0, keepdims=True)
    term_re, term_im = columns_forward(receive_one(2))
    middle_re = decay * state_re + phi_one * term_re
    middle_im = decay * state_im + phi_one * term_im

    toward_x = columns_inverse(-deriv_x * middle_im, deriv_x * middle_re)
    toward_y = columns_inverse(-deriv_y * middle_im, deriv_y * middle_re)
    pack([toward_x, toward_y], pair_out, 0)
    send(pair_out, pair_in, 0, 5, other)
    basis_spectra(3)
    offset = (freq_x * shift_ref[0] + freq_y * shift_ref[1]) & (GRID - 1)
    angle = (2.0 * math.pi / GRID) * offset.astype(f32)
    is_last = other == SEGS - 1
    cosine = jnp.where(is_last, jnp.cos(angle), 1.0)
    sine = jnp.where(is_last, jnp.sin(angle), 0.0)
    arrival(pair_out, pair_in, 0, 5).wait_recv()
    got_x, got_y = received(pair_in, 0, 2)
    term = -(grad[2].astype(f32) * rows_inverse(got_x) + grad[3].astype(f32) * rows_inverse(got_y))

    send_one(rows_forward(term), 3, other)
    kept_re = middle_re - phi_two * term_re
    kept_im = middle_im - phi_two * term_im
    term_re, term_im = columns_forward(receive_one(3))
    state_re = kept_re + phi_two * term_re
    state_im = kept_im + phi_two * term_im

    flow = columns_inverse(cosine * state_re + sine * state_im, cosine * state_im - sine * state_re)
    pl.semaphore_wait(ready, 1)
    send_one(flow, 4, after)
    flow = receive_one(4)

    def folded(value):
        total = value[:8]
        for at in range(1, 32):
            total = total + value[8 * at : 8 * at + 8]
        return jnp.sum(total, axis=0, keepdims=True)

    lines = [folded(flow * spectra[at]) for at in range(KRYLOV)]
    lines.append(folded(flow * flow * weight))
    lines.append(jnp.zeros((7, 128), f32))
    sums = jnp.sum(jnp.concatenate(lines, axis=0), axis=1, keepdims=True)
    spot_row = lax.broadcasted_iota(jnp.int32, (16, 128), 0)
    spot_lane = lax.broadcasted_iota(jnp.int32, (16, 128), 1)
    line = jnp.sum(jnp.where(spot_row == spot_lane, sums, 0.0), axis=0, keepdims=True) + gram_sums

    def spread(target, peers_of, own, count, at):
        target[own] = mine[at]

        def send_to(peers):
            for peer in peers:
                pltpu.make_async_remote_copy(
                    src_ref=mine.at[at],
                    dst_ref=target.at[own],
                    send_sem=send_sem.at[6 + at],
                    recv_sem=recv_sem.at[6 + at],
                    device_id=peer,
                    device_id_type=MESH,
                ).start()

        def step_to(step, carry):
            send_to(peers_of(step))
            return carry

        lax.fori_loop(0, 7, step_to, 0)
        send_to(peers_of(7)[:-1])
        return pltpu.make_async_remote_copy(
            src_ref=target.at[pl.ds(0, count - 1)],
            dst_ref=target.at[pl.ds(0, count - 1)],
            send_sem=send_sem.at[6 + at],
            recv_sem=recv_sem.at[6 + at],
            device_id={"seg": other},
            device_id_type=MESH,
        )

    mine[0] = line
    sent_a = spread(sum_a, peers_in_column, place, COLUMN, 0)
    wrapped = rows_inverse(flow) - start
    sent_a.wait_recv()
    mine[1] = jnp.sum(sum_a[...], axis=0)
    sent_b = spread(sum_b, peers_in_plane, 8 * chip_x + chip_z, PLANE, 1)
    sent_b.wait_recv()
    line = jnp.sum(sum_b[...], axis=0) * (1.0 / (SEGS * GRID * GRID))

    lanes = lax.broadcasted_iota(jnp.int32, (1, 128), 1)

    def lane_of(*signed_places):
        value = jnp.zeros((1, 128), f32)
        for sign, at in signed_places:
            value = value + jnp.where(lanes == at, sign * line, 0.0)
        return jnp.sum(value, axis=1, keepdims=True)

    coeffs = [lane_of((1.0, at), (-1.0, 16 + 8 * at + 7)) for at in range(KRYLOV)]
    norm_sq = lane_of((1.0, KRYLOV), (-2.0, KRYLOV - 1), (1.0, 79))
    left = jnp.zeros((1, 128), f32)
    right = jnp.zeros((1, 128), f32)
    for at in range(KRYLOV):
        left = left + jnp.where((lanes >= 16 + 8 * at) & (lanes < 24 + 8 * at), coeffs[at], 0.0)
        right = right + jnp.where((lanes >= 16) & (lanes % 8 == at) & (lanes < 80), coeffs[at], 0.0)
        norm_sq = norm_sq - 2.0 * coeffs[at] * coeffs[at]
    norm_sq = norm_sq + jnp.sum(left * right * line, axis=1, keepdims=True)
    norm = jnp.sqrt(norm_sq)
    column = jnp.where(lanes == KRYLOV, norm, 0.0)
    for at in range(KRYLOV):
        column = jnp.where(lanes == at, coeffs[at], column)
    hess_ref[...] = column
    inverse = 1.0 / norm
    remainder = wrapped
    for at in range(KRYLOV):
        remainder = remainder - coeffs[at] * basis[at].astype(f32)
    out_ref[0] = remainder * inverse

    for at in range(5):
        arrival(ones_out, ones_in, at, at).wait_send()
    arrival(pair_out, pair_in, 0, 5).wait_send()
    sent_a.wait_send()
    sent_b.wait_send()
    count_copy.wait_send()


def per_device(basis, base_grad, step_counts, shift):
    any_space = pl.BlockSpec(memory_space=pl.ANY)
    scalars = pl.BlockSpec(memory_space=pltpu.SMEM)
    f32, bf16 = jnp.float32, jnp.bfloat16
    new_vector, line = pl.pallas_call(
        kernel,
        out_shape=(
            jax.ShapeDtypeStruct((1, ROWS, GRID), f32),
            jax.ShapeDtypeStruct((1, 128), f32),
        ),
        grid_spec=pltpu.PrefetchScalarGridSpec(
            num_scalar_prefetch=2,
            grid=(),
            in_specs=[any_space] * 4,
            out_specs=(pl.BlockSpec(memory_space=pltpu.VMEM),) * 2,
            scratch_shapes=[
            pltpu.VMEM((KRYLOV, ROWS, GRID), bf16),
            pltpu.VMEM((4, ROWS, GRID), bf16),
            pltpu.VMEM(TABLE.shape, bf16),
            pltpu.VMEM((96, 128), f32),
            pltpu.VMEM((2, 1, 128), jnp.int32),
            pltpu.VMEM((5, SPACE, 5, 128), jnp.int32),
            pltpu.VMEM((5, SPACE, 5, 128), jnp.int32),
            pltpu.VMEM((1, SPACE, 10, 128), jnp.int32),
            pltpu.VMEM((1, SPACE, 10, 128), jnp.int32),
            pltpu.VMEM((KRYLOV, 256, 128), f32),
            pltpu.VMEM((2, 1, 128), f32),
            pltpu.VMEM((COLUMN, 1, 128), f32),
            pltpu.VMEM((PLANE, 1, 128), f32),
            pltpu.SemaphoreType.DMA((4,)),
            pltpu.SemaphoreType.DMA((9,)),
            pltpu.SemaphoreType.DMA((9,)),
            pltpu.SemaphoreType.REGULAR,
            pltpu.SemaphoreType.REGULAR,
        ],
        ),
        compiler_params=pltpu.CompilerParams(
            collective_id=0, has_side_effects=True, vmem_limit_bytes=54976 * 1024
        ),
    )(
        step_counts,
        shift,
        basis[0],
        base_grad.reshape(4, ROWS, GRID),
        jnp.asarray(TABLE),
        jnp.asarray(TWIST),
    )
    return new_vector, line[0, : KRYLOV + 1]


def solution(mesh):
    in_specs = (P("seg", None, "space", None), P("seg", None, None, "space", None), P("seg"), P())
    out_specs = (P("seg", "space", None), P())
    return jax.shard_map(
        per_device, mesh=mesh, in_specs=in_specs, out_specs=out_specs, check_vma=False
    )
```
